32 devices in a mesh: tx: 4 (over x, core), img: 8 (over z, y).
Axes of the slice: x: 2, y: 2, z: 4, core: 2. Of those that a mesh axis runs over, the one named last changes fastest.
Arguments:
- encoded: bfloat16 [1024, 1024, 512], P('tx', 'img'), may hold values from -6 to 6
- signs: int32 [1024, 64], replicated, may hold values from -1 to 1, as said below
- tx_block: int32 [64, 2048], P('tx'), may hold values from 0 to 1
- rx_block: int32 [1024, 2048], P(None, 'img'), may hold values from 0 to 2
- apodization: int32 [1024, 2048], P(None, 'img'), may hold values 0 or 1
Outputs:
- image: float32 [2048, 128], P('img', 'tx')
The draws below stay inside these ranges and needn't reach their ends.
Inputs may be any that keep to these rules, and one draw needn't show every extreme that they name: `signs`: every entry is 1 or -1. The columns are 64 distinct columns of the Sylvester Hadamard matrix of order 1024, every row multiplied by its own sign, so that two different columns are orthogonal.
All inputs are finite; a program needn't handle non-finite values. No bound on the sum of `apodization` on one device may be relied on, other than what follows from the above.
Results may differ from the reference program's by a relative error of at most 0.0029.
Values may be sent and summed in bfloat16 or wider, within the bound.
No kernel may reach another device: no remote copies, remote signals or barrier semaphores. Data moves between devices by JAX's collectives and lax.ppermute only.
A program may use at most 192 MiB of HBM per device.

```python
import math
import jax
import jax.numpy as jnp
from jax import lax

E = 1024
K = 64
R = 1024
NB = 4
L = 128
LINE_DEV = 256
LINES = 2048
N_IMG = 8


def draw_signs(key, part):
    key_cols = jax.random.fold_in(key, 11)
    key_rows = jax.random.fold_in(key, 23)
    columns = jax.random.permutation(key_cols, E)[:K].astype(jnp.int32)
    row_flips = jax.random.randint(key_rows, (E,), 0, 2).astype(jnp.int32) * 2 - 1
    events = jnp.arange(E, dtype=jnp.int32)
    shared = jnp.bitwise_and(events[:, None], columns[None, :])
    parity = jnp.zeros((E, K), jnp.int32)
    for position in range(int(math.log2(E))):
        parity = parity + jnp.bitwise_and(jnp.right_shift(shared, position), 1)
    sign_value = 1 - 2 * jnp.bitwise_and(parity, 1)
    return (sign_value * row_flips[:, None]).astype(jnp.int32)


def touch_ends(result, own_key, least, top_value):
    longest = result.shape.index(max(result.shape))
    spots = []
    for shift in (0, 1):
        where = [jax.random.randint(jax.random.fold_in(own_key, axis), (), 0, length) for axis, length in enumerate(result.shape)]
        where[longest] = (where[longest] + shift) % result.shape[longest]
        spots.append(tuple(where))
    return result.at[spots[0]].set(least).at[spots[1]].set(top_value)


def shard_levels(key, extent, pieces, low, high):
    loudness = 1.0
    for dim, parts in pieces:
        heights = jax.random.uniform(jax.random.fold_in(jax.random.fold_in(key, 6), dim), (parts,), jnp.float32, low / len(pieces), high / len(pieces))
        loudness = loudness * jnp.repeat(jnp.exp(heights), extent[dim] // parts).reshape((-1,) + (1,) * (len(extent) - 1 - dim))
    return loudness


def normal_values(own_key, extent, deviation, limit, shards=(), held_as=jnp.bfloat16):
    array = deviation * jax.random.normal(own_key, extent, jnp.float32)
    if shards:
        array = array * shard_levels(own_key, extent, shards, -0.22, 0.18)
    return jnp.clip(array, -limit, limit).astype(held_as)


def setup_inputs(seed: int = 0) -> dict:
    key_list = jax.random.split(jax.random.key(seed), 6)
    return {
        "encoded": normal_values(key_list[0], (E, R, NB * L), 1.0, 6.0, ((0, 4), (1, 8))),
        "signs": draw_signs(jax.random.fold_in(key_list[5], 71), 0),
        "tx_block": touch_ends(jax.random.randint(key_list[2], (K, LINES), 0, NB // 2), jax.random.fold_in(key_list[2], 1), 0, (NB // 2) - 1).astype(jnp.int32),
        "rx_block": touch_ends(jax.random.randint(key_list[3], (R, LINES), 0, NB - NB // 2 + 1), jax.random.fold_in(key_list[3], 1), 0, (NB - NB // 2 + 1) - 1).astype(jnp.int32),
        "apodization": touch_ends((jax.random.randint(key_list[4], (R, LINES), 0, 4) < 3).astype(jnp.int32), jax.random.fold_in(key_list[4], 1), 0, 1),
    }


def reference(encoded, signs, tx_block, rx_block, apodization):
    flat = encoded.reshape(E, R * NB * L)
    summed = jnp.dot(signs.T.astype(jnp.bfloat16), flat, preferred_element_type=jnp.float32)
    decoded = (summed * (1.0 / E)).astype(jnp.bfloat16)
    trace_rows = decoded.astype(jnp.float32).reshape(K * R * NB, L)
    levels = jnp.arange(NB, dtype=jnp.int32)

    def one_group(start):
        tx_rows = lax.dynamic_slice_in_dim(tx_block, start, LINE_DEV, 1)
        rx_rows = lax.dynamic_slice_in_dim(rx_block, start, LINE_DEV, 1)
        mask_rows = lax.dynamic_slice_in_dim(apodization, start, LINE_DEV, 1)
        total_block = tx_rows.T[:, :, None] + rx_rows.T[:, None, :]
        chosen = total_block[..., None] == levels
        weight = jnp.where(chosen, mask_rows.T[:, None, :, None].astype(jnp.float32), 0.0)
        weight = weight.reshape(LINE_DEV, K * R * NB)
        return jnp.dot(weight, trace_rows, precision=lax.Precision.HIGHEST, preferred_element_type=jnp.float32)
    starts = jnp.arange(N_IMG, dtype=jnp.int32) * LINE_DEV
    lines = lax.map(one_group, starts).reshape(LINES, L)
    return lines * math.sqrt(E / (K * R))
```

```python
import functools
import math

import jax
import jax.numpy as jnp
from jax import lax
from jax.experimental import pallas as pl
from jax.experimental.pallas import tpu as pltpu
from jax.sharding import PartitionSpec as P

L = 128
G = 8
RB = 16


def decode_kernel(st_ref, enc_ref, delta_ref, dsum_ref, sk_ref, x_ref):
    transmits, events = st_ref.shape
    samples = enc_ref.shape[2]
    rows, depth = sk_ref.shape
    width = 256 // G

    @pl.when(pl.program_id(0) == 0)
    def _():
        up = (
            lax.broadcasted_iota(jnp.int32, (rows, transmits), 0) // G
            == lax.broadcasted_iota(jnp.int32, (rows, transmits), 1)
        )
        tall = jnp.dot(
            up.astype(jnp.float32).astype(jnp.bfloat16),
            st_ref[...],
            preferred_element_type=jnp.float32,
        ).astype(jnp.bfloat16)
        step = 512
        for at in range(0, depth, step):
            out = (
                lax.broadcasted_iota(jnp.int32, (events, step), 1) + at
            ) // G == lax.broadcasted_iota(jnp.int32, (events, step), 0)
            wide = jnp.dot(
                tall,
                out.astype(jnp.float32).astype(jnp.bfloat16),
                preferred_element_type=jnp.float32,
            )
            same = (
                lax.broadcasted_iota(jnp.int32, (rows, step), 0) % G
                == lax.broadcasted_iota(jnp.int32, (rows, step), 1) % G
            )
            sk_ref[:, at : at + step] = jnp.where(same, wide, 0.0).astype(jnp.bfloat16)

    for at in range(0, events, width):
        piece = enc_ref[at : at + width].astype(jnp.float32)
        for half in range(RB // G):
            x_ref[half, at * G : (at + width) * G, :] = (
                piece[:, half * G : (half + 1) * G, :]
                .reshape(width * G, samples)
                .astype(jnp.bfloat16)
            )
    for half in range(RB // G):
        d = jnp.dot(sk_ref[...], x_ref[half], preferred_element_type=jnp.float32)
        low, high = d[:, : samples - L], d[:, L:]
        delta = (high - low) * 0.5
        mean = ((high + low) * 0.5).reshape(transmits, G, samples - L)
        here = slice(half * G, (half + 1) * G)
        delta_ref[:, here, :] = delta.reshape(transmits, G, samples - L).astype(
            delta_ref.dtype
        )
        dsum_ref[here, :] = jnp.sum(mean, axis=0)


def decode(st, encoded):
    transmits, events = st.shape
    _, receivers, samples = encoded.shape
    diff = samples - L
    return pl.pallas_call(
        decode_kernel,
        grid=(receivers // RB,),
        in_specs=[
            pl.BlockSpec((transmits, events), lambda g: (0, 0)),
            pl.BlockSpec((events, RB, samples), lambda g: (0, g, 0)),
        ],
        out_specs=[
            pl.BlockSpec((transmits, RB, diff), lambda g: (0, g, 0)),
            pl.BlockSpec((RB, diff), lambda g: (g, 0)),
        ],
        out_shape=[
            jax.ShapeDtypeStruct((transmits, receivers, diff), jnp.bfloat16),
            jax.ShapeDtypeStruct((receivers, diff), jnp.float32),
        ],
        scratch_shapes=[
            pltpu.VMEM((transmits * G, events * G), jnp.bfloat16),
            pltpu.VMEM((RB // G, events * G, samples), jnp.bfloat16),
        ],
        compiler_params=pltpu.CompilerParams(vmem_limit_bytes=50 * 2**20),
        cost_estimate=pl.CostEstimate(
            flops=2 * transmits * events * receivers * samples * G,
            bytes_accessed=events * receivers * samples * 2
            + transmits * receivers * diff * 2,
            transcendentals=0,
        ),
    )(st, encoded)


def beam_kernel(
    scale, at_once, mask_ref, tx_ref, delta_ref, dsum_ref, out_ref,
    a_ref, s_ref, acc_ref, rhs_ref,
):
    levels = delta_ref.shape[2] // L
    receivers = delta_ref.shape[1]
    groups, _, _, lines_here = mask_ref.shape
    lines = groups * lines_here
    step = pl.program_id(1)
    rows = 256

    @pl.when(step == 0)
    def _():
        for g in range(groups):
            rx = mask_ref[g, 0].astype(jnp.float32).T
            on = mask_ref[g, 1].astype(jnp.float32).T
            here = slice(g * lines_here, (g + 1) * lines_here)
            parts = [jnp.where(rx == v, on, 0.0) for v in range(levels)]
            a_ref[here, :] = jnp.concatenate(parts, axis=1).astype(jnp.bfloat16)
        for v in range(levels):
            whole = dsum_ref[:, v * L : (v + 1) * L]
            first = whole.astype(jnp.bfloat16)
            here = slice(v * receivers, (v + 1) * receivers)
            rhs_ref[0, here, :L] = first
            rhs_ref[0, here, L:] = (whole - first.astype(jnp.float32)).astype(
                jnp.bfloat16
            )
        for at in range(0, lines, rows):
            here = slice(at, at + rows)
            y = jnp.dot(a_ref[here, :], rhs_ref[0], preferred_element_type=jnp.float32)
            acc_ref[here, :] = y[:, :L] + y[:, L:]
            t = tx_ref[:, here].astype(jnp.float32)
            pad = jnp.zeros((L - t.shape[0], rows), jnp.float32)
            s = (2.0 * jnp.concatenate([t, pad], axis=0) - 1.0).T
            for g in range(s_ref.shape[0]):
                s_ref[g, here, :] = s if g == 0 else pltpu.roll(s, L - g * at_once, 1)

    for pair in range(at_once // 2):
        for side in range(2):
            for v in range(levels):
                rhs_ref[
                    pair, v * receivers : (v + 1) * receivers, side * L : (side + 1) * L
                ] = delta_ref[2 * pair + side, :, v * L : (v + 1) * L]
    for at in range(0, lines, rows):
        here = slice(at, at + rows)
        acc = acc_ref[here, :]
        for pair in range(at_once // 2):
            y = jnp.dot(a_ref[here, :], rhs_ref[pair], preferred_element_type=jnp.float32)
            k = 2 * pair
            acc = acc + s_ref[step, here, k : k + 1] * y[:, :L]
            acc = acc + s_ref[step, here, k + 1 : k + 2] * y[:, L:]
        acc_ref[here, :] = acc

    @pl.when(step == pl.num_programs(1) - 1)
    def _():
        stripes, _, deep, _ = out_ref.shape
        for g in range(groups):
            turned = (acc_ref[g * lines_here : (g + 1) * lines_here, :] * scale).T
            for t in range(stripes):
                out_ref[t, g] = turned[t * deep : (t + 1) * deep, :].astype(out_ref.dtype)


def beamform(scale, stripes, masks, tx_bits, delta, dsum):
    groups, _, receivers, lines_here = masks.shape
    transmits, lines = tx_bits.shape
    diff = delta.shape[2]
    levels = diff // L
    at_once = 8
    some = min(groups, 8)
    block = some * lines_here
    return pl.pallas_call(
        functools.partial(beam_kernel, scale, at_once),
        grid=(groups // some, transmits // at_once),
        in_specs=[
            pl.BlockSpec((some, 2, receivers, lines_here), lambda p, k: (p, 0, 0, 0)),
            pl.BlockSpec((transmits, block), lambda p, k: (0, p)),
            pl.BlockSpec((at_once, receivers, diff), lambda p, k: (k, 0, 0)),
            pl.BlockSpec((receivers, diff), lambda p, k: (0, 0)),
        ],
        out_specs=pl.BlockSpec(
            (stripes, some, L // stripes, lines_here), lambda p, k: (0, p, 0, 0)
        ),
        out_shape=jax.ShapeDtypeStruct(
            (stripes, groups, L // stripes, lines_here), jnp.bfloat16
        ),
        scratch_shapes=[
            pltpu.VMEM((block, levels * receivers), jnp.bfloat16),
            pltpu.VMEM((transmits // at_once, block, L), jnp.float32),
            pltpu.VMEM((block, L), jnp.float32),
            pltpu.VMEM((at_once // 2, levels * receivers, 2 * L), jnp.bfloat16),
        ],
        compiler_params=pltpu.CompilerParams(vmem_limit_bytes=50 * 2**20),
        cost_estimate=pl.CostEstimate(
            flops=2 * transmits * levels * receivers * lines * L,
            bytes_accessed=transmits * receivers * diff * 2,
            transcendentals=0,
        ),
    )(masks, tx_bits, delta, dsum)


def on_device(sizes, encoded, signs, tx_block, rx_block, apodization):
    events_here, receivers_here, samples = encoded.shape
    lines_here = rx_block.shape[1]
    stripes, groups = sizes
    events, transmits = signs.shape
    receivers = rx_block.shape[0]
    st = lax.dynamic_slice_in_dim(
        signs.T, lax.axis_index("tx") * events_here, events_here, 1
    ).astype(jnp.bfloat16)
    split = (groups, receivers_here, lines_here)
    masks = jnp.stack(
        [rx_block.reshape(split), apodization.reshape(split)], axis=1
    ).astype(jnp.bfloat16)
    masks = lax.all_to_all(masks, "img", 0, 0, tiled=True)
    tx_bits = lax.all_gather(tx_block.astype(jnp.bfloat16), "tx", axis=0, tiled=True)
    delta, dsum = decode(st, encoded)
    scale = math.sqrt(events / (transmits * receivers)) / events
    parts = beamform(scale, stripes, masks, tx_bits, delta, dsum)
    deep = L // stripes
    parts = parts.reshape(stripes * groups, deep, lines_here)
    parts = lax.all_to_all(parts, ("tx", "img"), 0, 0, tiled=True)
    return jnp.sum(parts.astype(jnp.float32), axis=0).T


def solution(mesh):
    placed = (P("tx", "img", None), P(), P("tx", None), P(None, "img"), P(None, "img"))
    sizes = (mesh.shape["tx"], mesh.shape["img"])
    return jax.shard_map(
        functools.partial(on_device, sizes),
        mesh=mesh, in_specs=placed, out_specs=P("img", "tx"), check_vma=False,
    )
```

```python
import functools
import math

import jax
import jax.numpy as jnp
from jax import lax
from jax.experimental import pallas as pl
from jax.experimental.pallas import tpu as pltpu
from jax.sharding import PartitionSpec as P

L = 128
G = 4
HALF = 8
RB = 16
BF = jnp.bfloat16
F32 = jnp.float32


def iota(shape, axis):
    return lax.broadcasted_iota(jnp.int32, shape, axis)


def dot(a, b):
    return jnp.dot(a, b, preferred_element_type=F32)


def cast_kernel(rx_ref, on_ref, tx_ref, out_ref, bits_ref):
    out_ref[0, 0] = rx_ref[...].astype(BF)
    out_ref[0, 1] = on_ref[...].astype(BF)

    @pl.when(pl.program_id(0) == 0)
    def _():
        bits_ref[...] = tx_ref[...].astype(BF)


def cast(groups, rx_block, apodization, tx_block):
    receivers, lines_here = rx_block.shape
    here = receivers // groups
    whole = pl.BlockSpec(tx_block.shape, lambda i: (0, 0))
    part = pl.BlockSpec((here, lines_here), lambda i: (i, 0))
    return pl.pallas_call(
        cast_kernel,
        grid=(groups,),
        in_specs=[part, part, whole],
        out_specs=[
            pl.BlockSpec((1, 2, here, lines_here), lambda i: (i, 0, 0, 0)),
            whole,
        ],
        out_shape=[
            jax.ShapeDtypeStruct((groups, 2, here, lines_here), BF),
            jax.ShapeDtypeStruct(tx_block.shape, BF),
        ],
    )(rx_block, apodization, tx_block)


def decode_kernel(
    stripes, at_ref, st_ref, enc_ref, delta_ref, dsum_ref, sk_ref, even_ref, odd_ref
):
    transmits, events = st_ref.shape
    samples = enc_ref.shape[2]
    rows, depth = sk_ref.shape
    step = pl.program_id(0)
    width = 32
    first = iota((1, HALF, samples), 1) < G

    @pl.when(step == 0)
    def _():
        turn = at_ref[0] * (transmits // stripes)
        up = lax.rem(iota((rows, transmits), 0) // G + turn, transmits)
        up = (up == iota((rows, transmits), 1)).astype(F32).astype(BF)
        tall = dot(up, st_ref[...].astype(F32).astype(BF)).astype(BF)
        wide = 512
        for at in range(0, depth, wide):
            out = (iota((events, wide), 1) + at) // G == iota((events, wide), 0)
            spread = dot(tall, out.astype(F32).astype(BF))
            same = iota((rows, wide), 0) % G == iota((rows, wide), 1) % G
            sk_ref[:, at : at + wide] = jnp.where(same, spread, 0.0).astype(BF)

    def lay_out(x_ref, half, at):
        piece = enc_ref[at : at + width].astype(F32)
        piece = piece[:, half * HALF : (half + 1) * HALF, :]
        piece = piece.reshape(width // 2, 2, HALF, samples)
        a, b = piece[:, 0], piece[:, 1]
        here = slice(at * G, (at + width) * G)
        low = jnp.where(first, a, pltpu.roll(b, G, 1))
        high = jnp.where(first, pltpu.roll(a, G, 1), b)
        x_ref[0, here, :] = low.reshape(width * G, samples).astype(BF)
        x_ref[1, here, :] = high.reshape(width * G, samples).astype(BF)

    def both(x_to, half, x_from):
        count = events // width
        pieces = []
        for c in range(count):
            lay_out(x_to, half, c * width)
            for q in range(4 * c // count, 4 * (c + 1) // count):
                n = slice((q // 2) * samples // 2, (q // 2 + 1) * samples // 2)
                pieces.append(dot(sk_ref[...], x_from[q % 2, :, n]))
        whole = []
        first_half = iota((1, HALF, samples // 2), 1) < G
        for low, high in ((pieces[0], pieces[1]), (pieces[2], pieces[3])):
            low = low.reshape(transmits // 2, HALF, samples // 2)
            high = high.reshape(transmits // 2, HALF, samples // 2)
            a = jnp.where(first_half, low, pltpu.roll(high, G, 1))
            b = jnp.where(first_half, pltpu.roll(low, G, 1), high)
            whole.append((a, b))
        blocks = [
            [side[..., n * L : (n + 1) * L] for n in range(samples // 2 // L)]
            for pair in whole
            for side in pair
        ]
        half_count = samples // 2 // L
        d = [
            [blocks[2 * (n // half_count) + odd][n % half_count] for odd in range(2)]
            for n in range(samples // L)
        ]
        for v in range(samples // L - 1):
            here = slice(v * L, (v + 1) * L)
            total = 0.0
            for odd in range(2):
                delta_ref[:, odd, :, here] = (d[v + 1][odd] - d[v][odd]) * 0.5
                total = total + jnp.sum(d[v + 1][odd] + d[v][odd], axis=0)
            dsum_ref[:, here] = total * 0.5

    @pl.when(step % 2 == 0)
    def _():
        both(even_ref, 0, odd_ref)

    @pl.when(step % 2 == 1)
    def _():
        both(odd_ref, 1, even_ref)


def decode(stripes, at, signs_t, encoded):
    transmits = signs_t.shape[0]
    events, receivers, samples = encoded.shape
    diff = samples - L
    steps = receivers // HALF
    blocks = receivers // RB
    shown = pltpu.PrefetchScalarGridSpec(
        num_scalar_prefetch=1,
        grid=(steps + 1,),
        in_specs=[
            pl.BlockSpec((transmits, events), lambda g, at: (0, at[0])),
            pl.BlockSpec(
                (events, RB, samples),
                lambda g, at: (0, jnp.minimum(g // (RB // HALF), blocks - 1), 0),
            ),
        ],
        out_specs=[
            pl.BlockSpec(
                (transmits // 2, 2, HALF, diff),
                lambda g, at: (0, 0, jnp.maximum(g - 1, 0), 0),
            ),
            pl.BlockSpec((HALF, diff), lambda g, at: (jnp.maximum(g - 1, 0), 0)),
        ],
        scratch_shapes=[
            pltpu.VMEM((transmits * G, events * G), BF),
            pltpu.VMEM((HALF // G, events * G, samples), BF),
            pltpu.VMEM((HALF // G, events * G, samples), BF),
        ],
    )
    return pl.pallas_call(
        functools.partial(decode_kernel, stripes),
        grid_spec=shown,
        out_shape=[
            jax.ShapeDtypeStruct((transmits // 2, 2, receivers, diff), F32),
            jax.ShapeDtypeStruct((receivers, diff), F32),
        ],
        compiler_params=pltpu.CompilerParams(vmem_limit_bytes=50 * 2**20),
        cost_estimate=pl.CostEstimate(
            flops=2 * transmits * events * receivers * samples * G,
            bytes_accessed=events * receivers * samples * 2
            + transmits * receivers * diff * 4,
            transcendentals=0,
        ),
    )(at, signs_t, encoded)


def beam_kernel(scale, at_once, mask_ref, delta_ref, dsum_ref, *refs):
    *tx_refs, out_ref, a_ref, s_ref, acc_ref, rhs_ref = refs
    levels = delta_ref.shape[3] // L
    receivers = delta_ref.shape[2]
    groups, _, _, lines_here = mask_ref.shape
    lines = groups * lines_here
    step = pl.program_id(1)
    rows = 256

    @pl.when(step == 0)
    def _():
        for v in range(levels):
            whole = dsum_ref[:, v * L : (v + 1) * L]
            high = whole.astype(BF)
            here = slice(v * receivers, (v + 1) * receivers)
            rhs_ref[0, here, :L] = high
            rhs_ref[0, here, L:] = (whole - high.astype(F32)).astype(BF)
        for g in range(groups):
            rx, on = mask_ref[g, 0].astype(F32), mask_ref[g, 1].astype(F32)
            code = (on * (rx + 1.0)).T
            here = slice(g * lines_here, (g + 1) * lines_here)
            parts = [jnp.where(code == v + 1, 1.0, 0.0) for v in range(levels)]
            a_ref[here, :] = jnp.concatenate(parts, axis=1).astype(BF)
        for at in range(0, lines, rows):
            here = slice(at, at + rows)
            y = dot(a_ref[here, :], rhs_ref[0])
            acc_ref[here, :] = y[:, :L] + y[:, L:]
            t = jnp.concatenate([ref[:, here].astype(F32) for ref in tx_refs], axis=0)
            pad = jnp.zeros((L - t.shape[0], rows), F32)
            s_ref[here, :] = (2.0 * jnp.concatenate([t, pad], axis=0) - 1.0).T

    for pair in range(at_once // 2):
        for side in range(2):
            for v in range(levels):
                rhs_ref[
                    pair, v * receivers : (v + 1) * receivers, side * L : (side + 1) * L
                ] = delta_ref[pair, side, :, v * L : (v + 1) * L].astype(BF)
    for at in range(0, lines, rows):
        here = slice(at, at + rows)
        acc = acc_ref[here, :]
        s = pltpu.roll(s_ref[here, :], L - step * at_once, 1)
        for pair in range(at_once // 2):
            y = dot(a_ref[here, :], rhs_ref[pair])
            k = 2 * pair
            acc = acc + s[:, k : k + 1] * y[:, :L]
            acc = acc + s[:, k + 1 : k + 2] * y[:, L:]
        acc_ref[here, :] = acc

    @pl.when(step == pl.num_programs(1) - 1)
    def _():
        stripes, _, deep, _ = out_ref.shape
        for g in range(groups):
            turned = (acc_ref[g * lines_here : (g + 1) * lines_here, :] * scale).T
            for t in range(stripes):
                out_ref[t, g] = turned[t * deep : (t + 1) * deep, :].astype(BF)


def beamform(scale, stripes, masks, tx_bits, delta, dsum):
    groups, _, receivers, lines_here = masks.shape
    pairs, _, _, diff = delta.shape
    levels = diff // L
    at_once = 8
    some = min(groups, 8)
    block = some * lines_here
    return pl.pallas_call(
        functools.partial(beam_kernel, scale, at_once),
        grid=(groups // some, 2 * pairs // at_once),
        in_specs=[
            pl.BlockSpec((some, 2, receivers, lines_here), lambda p, k: (p, 0, 0, 0)),
            pl.BlockSpec((at_once // 2, 2, receivers, diff), lambda p, k: (k, 0, 0, 0)),
            pl.BlockSpec((receivers, diff), lambda p, k: (0, 0)),
        ]
        + [pl.BlockSpec((t.shape[0], block), lambda p, k: (0, p)) for t in tx_bits],
        out_specs=pl.BlockSpec(
            (stripes, some, L // stripes, lines_here), lambda p, k: (0, p, 0, 0)
        ),
        out_shape=jax.ShapeDtypeStruct(
            (stripes, groups, L // stripes, lines_here), BF
        ),
        scratch_shapes=[
            pltpu.VMEM((block, levels * receivers), BF),
            pltpu.VMEM((block, L), F32),
            pltpu.VMEM((block, L), F32),
            pltpu.VMEM((at_once // 2, levels * receivers, 2 * L), BF),
        ],
        compiler_params=pltpu.CompilerParams(vmem_limit_bytes=50 * 2**20),
        cost_estimate=pl.CostEstimate(
            flops=4 * pairs * levels * receivers * groups * lines_here * L,
            bytes_accessed=2 * pairs * receivers * diff * 4,
            transcendentals=0,
        ),
    )(masks, delta, dsum, *tx_bits)


def on_device(sizes, encoded, signs, tx_block, rx_block, apodization):
    lines_here = rx_block.shape[1]
    stripes, groups = sizes
    events, transmits = signs.shape
    receivers = rx_block.shape[0]
    masks, own = cast(groups, rx_block, apodization, tx_block)
    masks = lax.all_to_all(masks, "img", 0, 0, tiled=True)
    tx_bits = [own] + [
        lax.ppermute(own, "tx", [((t + d) % stripes, t) for t in range(stripes)])
        for d in range(1, stripes)
    ]
    at = lax.axis_index("tx").astype(jnp.int32).reshape(1)
    delta, dsum = decode(stripes, at, signs.T, encoded)
    scale = math.sqrt(events / (transmits * receivers)) / events
    parts = beamform(scale, stripes, masks, tx_bits, delta, dsum)
    parts = parts.reshape(stripes * groups, L // stripes, lines_here)
    parts = lax.all_to_all(parts, ("tx", "img"), 0, 0, tiled=True)
    return jnp.sum(parts.astype(F32), axis=0).T


def solution(mesh):
    placed = (P("tx", "img", None), P(), P("tx", None), P(None, "img"), P(None, "img"))
    sizes = (mesh.shape["tx"], mesh.shape["img"])
    return jax.shard_map(
        functools.partial(on_device, sizes),
        mesh=mesh, in_specs=placed, out_specs=P("img", "tx"), check_vma=False,
    )
```

```python
import functools
import math

import jax
import jax.numpy as jnp
from jax import lax
from jax.experimental import pallas as pl
from jax.experimental.pallas import tpu as pltpu
from jax.sharding import PartitionSpec as P

L = 128
G = 8
RB = 16
BF = jnp.bfloat16
F32 = jnp.float32


def iota(shape, axis):
    return lax.broadcasted_iota(jnp.int32, shape, axis)


def dot(a, b):
    return jnp.dot(a, b, preferred_element_type=F32)


def cast_kernel(rx_ref, on_ref, tx_ref, out_ref, bits_ref):
    out_ref[:, 0] = rx_ref[...].astype(F32).astype(BF)
    out_ref[:, 1] = on_ref[...].astype(F32).astype(BF)

    @pl.when(pl.program_id(0) == 0)
    def _():
        bits_ref[...] = tx_ref[...].astype(F32).astype(BF)


def cast(groups, rx_block, apodization, tx_block):
    receivers, lines_here = rx_block.shape
    here = receivers // groups
    split = (groups, here, lines_here)
    whole = pl.BlockSpec(tx_block.shape, lambda i: (0, 0))
    part = pl.BlockSpec((groups // 2, here, lines_here), lambda i: (i, 0, 0))
    return pl.pallas_call(
        cast_kernel,
        grid=(2,),
        in_specs=[part, part, whole],
        out_specs=[
            pl.BlockSpec((groups // 2, 2, here, lines_here), lambda i: (i, 0, 0, 0)),
            whole,
        ],
        out_shape=[
            jax.ShapeDtypeStruct((groups, 2, here, lines_here), BF),
            jax.ShapeDtypeStruct(tx_block.shape, BF),
        ],
    )(rx_block.reshape(split), apodization.reshape(split), tx_block)


def decode_kernel(
    stripes, at_ref, st_ref, enc_ref, delta_ref, dsum_ref,
    sk_ref, even_ref, odd_ref, held_ref,
):
    transmits, events = st_ref.shape
    samples = enc_ref.shape[2]
    rows, depth = sk_ref.shape
    step, last = pl.program_id(0), pl.num_programs(0) - 1
    width = 32
    count = events // width
    levels = samples // L - 1

    def lay_out(x_ref, half, c):
        piece = enc_ref[c * width : (c + 1) * width].astype(F32)
        piece = piece[:, half * G : (half + 1) * G, :]
        here = slice(c * width * G, (c + 1) * width * G)
        x_ref[here, :] = piece.reshape(width * G, samples).astype(BF)

    def product(x_to, half, x_from):
        blocks = []
        for c in range(count):
            lay_out(x_to, half, c)
            for q in range(2 * c // count, 2 * (c + 1) // count):
                n = slice(q * samples // 2, (q + 1) * samples // 2)
                d = dot(sk_ref[...], x_from[:, n]).reshape(transmits, G, samples // 2)
                blocks += [d[..., at : at + L] for at in range(0, samples // 2, L)]
        delta = [(blocks[v + 1] - blocks[v]) * 0.5 for v in range(levels)]
        mean = [
            jnp.sum(blocks[v + 1] + blocks[v], axis=0) * 0.5 for v in range(levels)
        ]
        return delta, mean

    @pl.when(step == 0)
    def _():
        turn = at_ref[0] * (transmits // stripes)
        up = lax.rem(iota((rows, transmits), 0) // G + turn, transmits)
        up = (up == iota((rows, transmits), 1)).astype(F32).astype(BF)
        tall = dot(up, st_ref[...].astype(F32).astype(BF)).astype(BF)
        wide = 512
        for at in range(0, depth, wide):
            out = (iota((events, wide), 1) + at) // G == iota((events, wide), 0)
            spread = dot(tall, out.astype(F32).astype(BF))
            same = iota((rows, wide), 0) % G == iota((rows, wide), 1) % G
            sk_ref[:, at : at + wide] = jnp.where(same, spread, 0.0).astype(BF)
        for c in range(count):
            lay_out(even_ref, 0, c)

    @pl.when(step > 0)
    def _():
        delta, mean = product(even_ref, 0, odd_ref)
        for v in range(levels):
            here = slice(v * L, (v + 1) * L)
            delta_ref[:, :, here] = jnp.concatenate(
                [held_ref[:transmits, :, here], delta[v]], axis=1
            ).astype(BF)
            dsum_ref[:G, here] = held_ref[transmits, :, here]
            dsum_ref[G:, here] = mean[v]

    @pl.when(step < last)
    def _():
        delta, mean = product(odd_ref, 1, even_ref)
        for v in range(levels):
            here = slice(v * L, (v + 1) * L)
            held_ref[:transmits, :, here] = delta[v]
            held_ref[transmits, :, here] = mean[v]


def decode(stripes, at, signs_t, encoded):
    transmits = signs_t.shape[0]
    events, receivers, samples = encoded.shape
    diff = samples - L
    blocks = receivers // RB
    shown = pltpu.PrefetchScalarGridSpec(
        num_scalar_prefetch=1,
        grid=(blocks + 1,),
        in_specs=[
            pl.BlockSpec((transmits, events), lambda g, at: (0, at[0])),
            pl.BlockSpec(
                (events, RB, samples), lambda g, at: (0, jnp.minimum(g, blocks - 1), 0)
            ),
        ],
        out_specs=[
            pl.BlockSpec(
                (transmits, RB, diff), lambda g, at: (0, jnp.maximum(g - 1, 0), 0)
            ),
            pl.BlockSpec((RB, diff), lambda g, at: (jnp.maximum(g - 1, 0), 0)),
        ],
        scratch_shapes=[
            pltpu.VMEM((transmits * G, events * G), BF),
            pltpu.VMEM((events * G, samples), BF),
            pltpu.VMEM((events * G, samples), BF),
            pltpu.VMEM((transmits + 1, G, diff), F32),
        ],
    )
    return pl.pallas_call(
        functools.partial(decode_kernel, stripes),
        grid_spec=shown,
        out_shape=[
            jax.ShapeDtypeStruct((transmits, receivers, diff), BF),
            jax.ShapeDtypeStruct((receivers, diff), F32),
        ],
        compiler_params=pltpu.CompilerParams(vmem_limit_bytes=50 * 2**20),
        cost_estimate=pl.CostEstimate(
            flops=2 * transmits * events * receivers * samples * G,
            bytes_accessed=events * receivers * samples * 2
            + transmits * receivers * diff * 2,
            transcendentals=0,
        ),
    )(at, signs_t, encoded)


def beam_kernel(scale, mask_ref, delta_ref, dsum_ref, *refs):
    *tx_refs, out_ref, a_ref, s_ref, acc_ref, even_ref, odd_ref = refs
    block, receivers, diff = delta_ref.shape
    levels = diff // L
    half = block // 2
    groups, _, _, wide = mask_ref.shape
    step, last = pl.program_id(1), pl.num_programs(1) - 1

    def turn(x_to, side, k):
        for v in range(levels):
            x_to[k * L : (k + 1) * L, v * receivers : (v + 1) * receivers] = delta_ref[
                side * half + k, :, v * L : (v + 1) * L
            ].T

    def product(x_from, k0, beside):
        for g in range(groups):
            for k in range(g * half // groups, (g + 1) * half // groups):
                beside(k)
            here = slice(g * wide, (g + 1) * wide)
            y = dot(x_from[...], a_ref[:, here]).reshape(half, L // 8, 8, wide)
            acc = acc_ref[:, :, here]
            for k in range(half):
                acc = acc + s_ref[k0 + k, :, here] * y[k]
            acc_ref[:, :, here] = acc

    @pl.when(step == 0)
    def _():
        for v in range(levels):
            whole = dsum_ref[:, v * L : (v + 1) * L]
            high = whole.astype(BF)
            here = slice(v * receivers, (v + 1) * receivers)
            odd_ref[:L, here] = high.T
            odd_ref[L : 2 * L, here] = (whole - high.astype(F32)).astype(BF).T
        for g in range(groups):
            here = slice(g * wide, (g + 1) * wide)
            rx, on = mask_ref[g, 0].astype(F32), mask_ref[g, 1].astype(F32)
            for v in range(levels):
                a_ref[v * receivers : (v + 1) * receivers, here] = jnp.where(
                    rx == v, on, 0.0
                ).astype(BF)
            y = dot(odd_ref[: 2 * L, :], a_ref[:, here])
            acc_ref[:, :, here] = (y[:L] + y[L:]).reshape(L // 8, 8, wide)
            at = 0
            for ref in tx_refs:
                s = 2.0 * ref[:, here].astype(F32) - 1.0
                for k in range(ref.shape[0]):
                    s_ref[at + k, :, here] = jnp.broadcast_to(s[k : k + 1], (8, wide))
                at += ref.shape[0]
        for k in range(half):
            turn(even_ref, 0, k)

    @pl.when(step > 0)
    def _():
        product(odd_ref, step * block - half, functools.partial(turn, even_ref, 0))

    @pl.when(step < last)
    def _():
        product(even_ref, step * block, functools.partial(turn, odd_ref, 1))

    @pl.when(step == last)
    def _():
        stripes, _, deep, _ = out_ref.shape
        for g in range(groups):
            here = slice(g * wide, (g + 1) * wide)
            whole = (acc_ref[:, :, here] * scale).reshape(L, wide)
            for t in range(stripes):
                out_ref[t, g] = whole[t * deep : (t + 1) * deep, :].astype(BF)


def beamform(scale, stripes, masks, tx_bits, delta, dsum):
    groups, _, receivers, wide = masks.shape
    transmits, _, diff = delta.shape
    levels = diff // L
    block = 16
    some = min(groups, 8)
    steps = transmits // block
    return pl.pallas_call(
        functools.partial(beam_kernel, scale),
        grid=(groups // some, steps + 1),
        in_specs=[
            pl.BlockSpec((some, 2, receivers, wide), lambda p, k: (p, 0, 0, 0)),
            pl.BlockSpec(
                (block, receivers, diff), lambda p, k: (jnp.minimum(k, steps - 1), 0, 0)
            ),
            pl.BlockSpec((receivers, diff), lambda p, k: (0, 0)),
        ]
        + [
            pl.BlockSpec((t.shape[0], some * wide), lambda p, k: (0, p))
            for t in tx_bits
        ],
        out_specs=pl.BlockSpec(
            (stripes, some, L // stripes, wide), lambda p, k: (0, p, 0, 0)
        ),
        out_shape=jax.ShapeDtypeStruct((stripes, groups, L // stripes, wide), BF),
        scratch_shapes=[
            pltpu.VMEM((levels * receivers, some * wide), BF),
            pltpu.VMEM((transmits, 8, some * wide), F32),
            pltpu.VMEM((L // 8, 8, some * wide), F32),
            pltpu.VMEM((block // 2 * L, levels * receivers), BF),
            pltpu.VMEM((block // 2 * L, levels * receivers), BF),
        ],
        compiler_params=pltpu.CompilerParams(vmem_limit_bytes=50 * 2**20),
        cost_estimate=pl.CostEstimate(
            flops=2 * transmits * levels * receivers * groups * wide * L,
            bytes_accessed=transmits * receivers * diff * 2,
            transcendentals=0,
        ),
    )(masks, delta, dsum, *tx_bits)


def on_device(sizes, encoded, signs, tx_block, rx_block, apodization):
    lines_here = rx_block.shape[1]
    stripes, groups = sizes
    events, transmits = signs.shape
    receivers = rx_block.shape[0]
    masks, own = cast(groups, rx_block, apodization, tx_block)
    masks = lax.all_to_all(masks, "img", 0, 0, tiled=True)
    tx_bits = [own] + [
        lax.ppermute(own, "tx", [((t + d) % stripes, t) for t in range(stripes)])
        for d in range(1, stripes)
    ]
    at = lax.axis_index("tx").astype(jnp.int32).reshape(1)
    delta, dsum = decode(stripes, at, signs.T, encoded)
    scale = math.sqrt(events / (transmits * receivers)) / events
    parts = beamform(scale, stripes, masks, tx_bits, delta, dsum)
    parts = parts.reshape(stripes * groups, L // stripes, lines_here)
    parts = lax.all_to_all(parts, ("tx", "img"), 0, 0, tiled=True)
    return jnp.sum(parts.astype(F32), axis=0).T


def solution(mesh):
    placed = (P("tx", "img", None), P(), P("tx", None), P(None, "img"), P(None, "img"))
    sizes = (mesh.shape["tx"], mesh.shape["img"])
    return jax.shard_map(
        functools.partial(on_device, sizes),
        mesh=mesh, in_specs=placed, out_specs=P("img", "tx"), check_vma=False,
    )
```

```python
import functools
import math

import jax
import jax.numpy as jnp
from jax import lax
from jax.experimental import pallas as pl
from jax.experimental.pallas import tpu as pltpu
from jax.sharding import PartitionSpec as P

L = 128
G = 8
RB = 16
BF = jnp.bfloat16
F32 = jnp.float32


def iota(shape, axis):
    return lax.broadcasted_iota(jnp.int32, shape, axis)


def dot(a, b):
    return jnp.dot(a, b, preferred_element_type=F32)


def cast_kernel(rx_ref, on_ref, tx_ref, out_ref, bits_ref):
    out_ref[:, 0] = rx_ref[...].astype(F32).astype(BF)
    out_ref[:, 1] = on_ref[...].astype(F32).astype(BF)

    @pl.when(pl.program_id(0) == 0)
    def _():
        bits_ref[...] = tx_ref[...].astype(F32).astype(BF)


def cast(groups, rx_block, apodization, tx_block):
    receivers, lines_here = rx_block.shape
    here = receivers // groups
    split = (groups, here, lines_here)
    whole = pl.BlockSpec(tx_block.shape, lambda i: (0, 0))
    part = pl.BlockSpec((groups // 2, here, lines_here), lambda i: (i, 0, 0))
    return pl.pallas_call(
        cast_kernel,
        grid=(2,),
        in_specs=[part, part, whole],
        out_specs=[
            pl.BlockSpec((groups // 2, 2, here, lines_here), lambda i: (i, 0, 0, 0)),
            whole,
        ],
        out_shape=[
            jax.ShapeDtypeStruct((groups, 2, here, lines_here), BF),
            jax.ShapeDtypeStruct(tx_block.shape, BF),
        ],
    )(rx_block.reshape(split), apodization.reshape(split), tx_block)


def decode_kernel(
    stripes, at_ref, st_ref, enc_ref, delta_ref, dsum_ref, sk_ref, x_ref
):
    transmits = delta_ref.shape[0]
    every, events = st_ref.shape
    samples = enc_ref.shape[2]
    rows, depth = sk_ref.shape
    width = 32

    @pl.when(pl.program_id(0) == 0)
    def _():
        group = every // stripes
        row = iota((rows, every), 0) // G
        wanted = lax.rem(at_ref[1] + 2 * (row // group), stripes) * group + row % group
        up = (wanted == iota((rows, every), 1)).astype(F32).astype(BF)
        tall = dot(up, st_ref[...].astype(F32).astype(BF)).astype(BF)
        wide = 512
        for at in range(0, depth, wide):
            out = (iota((events, wide), 1) + at) // G == iota((events, wide), 0)
            spread = dot(tall, out.astype(F32).astype(BF))
            same = iota((rows, wide), 0) % G == iota((rows, wide), 1) % G
            sk_ref[:, at : at + wide] = jnp.where(same, spread, 0.0).astype(BF)

    for at in range(0, events, width):
        piece = enc_ref[at : at + width].astype(F32)
        for half in range(RB // G):
            x_ref[half, at * G : (at + width) * G, :] = (
                piece[:, half * G : (half + 1) * G, :]
                .reshape(width * G, samples)
                .astype(BF)
            )
    deltas = []
    for half in range(RB // G):
        d = dot(sk_ref[...], x_ref[half])
        low, high = d[:, : samples - L], d[:, L:]
        deltas.append(((high - low) * 0.5).reshape(transmits, G, samples - L))
        mean = (high + low).reshape(transmits, G, samples - L)
        dsum_ref[half * G : (half + 1) * G, :] = jnp.sum(mean, axis=0) * 0.5
    delta_ref[...] = jnp.concatenate(deltas, axis=1).astype(delta_ref.dtype)


def decode(stripes, kept, at, signs_t, encoded):
    every = signs_t.shape[0]
    transmits = every // 2
    events, receivers, samples = encoded.shape
    diff = samples - L
    shown = pltpu.PrefetchScalarGridSpec(
        num_scalar_prefetch=1,
        grid=(receivers // RB,),
        in_specs=[
            pl.BlockSpec((every, events), lambda g, at: (0, at[0])),
            pl.BlockSpec((events, RB, samples), lambda g, at: (0, g, 0)),
        ],
        out_specs=[
            pl.BlockSpec((transmits, RB, diff), lambda g, at: (0, g, 0)),
            pl.BlockSpec((RB, diff), lambda g, at: (g, 0)),
        ],
        scratch_shapes=[
            pltpu.VMEM((transmits * G, events * G), BF),
            pltpu.VMEM((RB // G, events * G, samples), BF),
        ],
    )
    return pl.pallas_call(
        functools.partial(decode_kernel, stripes),
        grid_spec=shown,
        out_shape=[
            jax.ShapeDtypeStruct((transmits, receivers, diff), kept),
            jax.ShapeDtypeStruct((receivers, diff), F32),
        ],
        compiler_params=pltpu.CompilerParams(vmem_limit_bytes=50 * 2**20),
        cost_estimate=pl.CostEstimate(
            flops=2 * transmits * events * receivers * samples * G,
            bytes_accessed=events * receivers * samples * 2
            + transmits * receivers * diff * 4,
            transcendentals=0,
        ),
    )(at, signs_t, encoded)


def beam_kernel(scale, mask_ref, own_ref, other_ref, mean1_ref, mean2_ref, *refs):
    *tx_refs, out_ref, a_ref, s_ref, acc_ref, even_ref, odd_ref = refs
    block, receivers, diff = own_ref.shape
    levels = diff // L
    half = block // 2
    groups, _, _, wide = mask_ref.shape
    step, last = pl.program_id(1), pl.num_programs(1) - 1

    def turn(x_to, side, k):
        for v in range(levels):
            here = slice(v * L, (v + 1) * L)
            whole = own_ref[side * half + k, :, here] + other_ref[
                side * half + k, :, here
            ].astype(F32)
            x_to[k * L : (k + 1) * L, v * receivers : (v + 1) * receivers] = (
                whole.astype(BF).T
            )

    def product(x_from, k0, beside):
        for g in range(groups):
            for k in range(g * half // groups, (g + 1) * half // groups):
                beside(k)
            here = slice(g * wide, (g + 1) * wide)
            y = dot(x_from[...], a_ref[:, here]).reshape(half, L // 8, 8, wide)
            acc = acc_ref[:, :, here]
            for k in range(half):
                acc = acc + s_ref[k0 + k, :, here] * y[k]
            acc_ref[:, :, here] = acc

    @pl.when(step == 0)
    def _():
        for v in range(levels):
            here = slice(v * L, (v + 1) * L)
            whole = mean1_ref[:, here] + mean2_ref[:, here]
            high = whole.astype(BF)
            here = slice(v * receivers, (v + 1) * receivers)
            odd_ref[:L, here] = high.T
            odd_ref[L : 2 * L, here] = (whole - high.astype(F32)).astype(BF).T
        for g in range(groups):
            here = slice(g * wide, (g + 1) * wide)
            rx, on = mask_ref[g, 0].astype(F32), mask_ref[g, 1].astype(F32)
            for v in range(levels):
                a_ref[v * receivers : (v + 1) * receivers, here] = jnp.where(
                    rx == v, on, 0.0
                ).astype(BF)
            y = dot(odd_ref[: 2 * L, :], a_ref[:, here])
            acc_ref[:, :, here] = (y[:L] + y[L:]).reshape(L // 8, 8, wide)
            at = 0
            for ref in tx_refs:
                s = 2.0 * ref[:, here].astype(F32) - 1.0
                for k in range(ref.shape[0]):
                    s_ref[at + k, :, here] = jnp.broadcast_to(s[k : k + 1], (8, wide))
                at += ref.shape[0]
        for k in range(half):
            turn(even_ref, 0, k)

    @pl.when(step > 0)
    def _():
        product(odd_ref, step * block - half, functools.partial(turn, even_ref, 0))

    @pl.when(step < last)
    def _():
        product(even_ref, step * block, functools.partial(turn, odd_ref, 1))

    @pl.when(step == last)
    def _():
        stripes, _, deep, _ = out_ref.shape
        for g in range(groups):
            here = slice(g * wide, (g + 1) * wide)
            whole = (acc_ref[:, :, here] * scale).reshape(L, wide)
            for t in range(stripes):
                out_ref[t, g] = whole[t * deep : (t + 1) * deep, :].astype(BF)


def beamform(scale, stripes, masks, tx_bits, own, other, mean1, mean2):
    groups, _, receivers, wide = masks.shape
    transmits, _, diff = own.shape
    levels = diff // L
    block = 16
    some = min(groups, 8)
    steps = transmits // block
    part = pl.BlockSpec(
        (block, receivers, diff), lambda p, k: (jnp.minimum(k, steps - 1), 0, 0)
    )
    mean = pl.BlockSpec((receivers, diff), lambda p, k: (0, 0))
    return pl.pallas_call(
        functools.partial(beam_kernel, scale),
        grid=(groups // some, steps + 1),
        in_specs=[
            pl.BlockSpec((some, 2, receivers, wide), lambda p, k: (p, 0, 0, 0)),
            part,
            part,
            mean,
            mean,
        ]
        + [
            pl.BlockSpec((t.shape[0], some * wide), lambda p, k: (0, p))
            for t in tx_bits
        ],
        out_specs=pl.BlockSpec(
            (stripes, some, L // stripes, wide), lambda p, k: (0, p, 0, 0)
        ),
        out_shape=jax.ShapeDtypeStruct((stripes, groups, L // stripes, wide), BF),
        scratch_shapes=[
            pltpu.VMEM((levels * receivers, some * wide), BF),
            pltpu.VMEM((transmits, 8, some * wide), F32),
            pltpu.VMEM((L // 8, 8, some * wide), F32),
            pltpu.VMEM((block // 2 * L, levels * receivers), BF),
            pltpu.VMEM((block // 2 * L, levels * receivers), BF),
        ],
        compiler_params=pltpu.CompilerParams(vmem_limit_bytes=50 * 2**20),
        cost_estimate=pl.CostEstimate(
            flops=2 * transmits * levels * receivers * groups * wide * L,
            bytes_accessed=transmits * receivers * diff * 6,
            transcendentals=0,
        ),
    )(masks, own, other, mean1, mean2, *tx_bits)


def on_device(sizes, encoded, signs, tx_block, rx_block, apodization):
    lines_here = rx_block.shape[1]
    stripes, groups = sizes
    events, transmits = signs.shape
    receivers = rx_block.shape[0]
    masks, own = cast(groups, rx_block, apodization, tx_block)
    masks = lax.all_to_all(masks, "img", 0, 0, tiled=True)
    tx_bits = [own] + [
        lax.ppermute(own, "tx", [((t + d) % stripes, t) for t in range(stripes)])
        for d in range(2, stripes, 2)
    ]
    t = lax.axis_index("tx").astype(jnp.int32)
    pair = t + 1 - 2 * lax.rem(t, 2)
    signs_t = signs.T
    theirs, mean1 = decode(stripes, BF, jnp.stack([t, pair]), signs_t, encoded)
    theirs = lax.ppermute(theirs, "tx", [(t, t ^ 1) for t in range(stripes)])
    ours, mean2 = decode(stripes, F32, jnp.stack([t, t]), signs_t, encoded)
    scale = math.sqrt(events / (transmits * receivers)) / events
    parts = beamform(scale, stripes, masks, tx_bits, ours, theirs, mean1, mean2)
    parts = parts.reshape(stripes * groups, L // stripes, lines_here)
    parts = lax.all_to_all(parts, ("tx", "img"), 0, 0, tiled=True)
    return jnp.sum(parts.astype(F32), axis=0).T


def solution(mesh):
    placed = (P("tx", "img", None), P(), P("tx", None), P(None, "img"), P(None, "img"))
    sizes = (mesh.shape["tx"], mesh.shape["img"])
    return jax.shard_map(
        functools.partial(on_device, sizes),
        mesh=mesh, in_specs=placed, out_specs=P("img", "tx"), check_vma=False,
    )
```

```python
import functools
import math

import jax
import jax.numpy as jnp
from jax import lax
from jax.experimental import pallas as pl
from jax.experimental.pallas import tpu as pltpu
from jax.sharding import PartitionSpec as P

L = 128
PITCH = 24
RB = 16
BF = jnp.bfloat16
F32 = jnp.float32


def iota(shape, axis):
    return lax.broadcasted_iota(jnp.int32, shape, axis)


def dot(a, b):
    return jnp.dot(a, b, preferred_element_type=F32)


def cast_kernel(
    stripes, at_ref, rx_ref, on_ref, tx_ref, sign_ref, out_ref, bits_ref, st_ref
):
    out_ref[:, 0] = rx_ref[...].astype(F32).astype(BF)
    out_ref[:, 1] = on_ref[...].astype(F32).astype(BF)

    @pl.when(pl.program_id(0) == 0)
    def _():
        bits_ref[...] = tx_ref[...].astype(F32).astype(BF)
        every = st_ref.shape[0]
        turn = at_ref[0] * (every // stripes)
        row = lax.rem(iota((every, every), 0) + turn, every)
        up = (row == iota((every, every), 1)).astype(F32).astype(BF)
        st_ref[...] = dot(up, sign_ref[...].astype(F32).astype(BF)).astype(BF)


def cast(sizes, at, rx_block, apodization, tx_block, signs_t):
    stripes, groups = sizes
    receivers, lines_here = rx_block.shape
    every, events = signs_t.shape
    here = receivers // groups
    split = (groups, here, lines_here)
    whole = pl.BlockSpec(tx_block.shape, lambda i, at: (0, 0))
    part = pl.BlockSpec((groups // 2, here, lines_here), lambda i, at: (i, 0, 0))
    return pl.pallas_call(
        functools.partial(cast_kernel, stripes),
        grid_spec=pltpu.PrefetchScalarGridSpec(
            num_scalar_prefetch=1,
            grid=(2,),
            in_specs=[
                part,
                part,
                whole,
                pl.BlockSpec((every, events // stripes), lambda i, at: (0, at[0])),
            ],
            out_specs=[
                pl.BlockSpec(
                    (groups // 2, 2, here, lines_here), lambda i, at: (i, 0, 0, 0)
                ),
                whole,
                pl.BlockSpec((every, events // stripes), lambda i, at: (0, 0)),
            ],
        ),
        out_shape=[
            jax.ShapeDtypeStruct((groups, 2, here, lines_here), BF),
            jax.ShapeDtypeStruct(tx_block.shape, BF),
            jax.ShapeDtypeStruct((every, events // stripes), BF),
        ],
    )(at, rx_block.reshape(split), apodization.reshape(split), tx_block, signs_t)


def decode_kernel(st_ref, enc_ref, delta_ref, dsum_ref, rows_ref, turn_ref):
    transmits, events = st_ref.shape
    samples = enc_ref.shape[2]
    parts, levels = samples // L, samples // L - 1
    for e in range(events):
        piece = enc_ref[e].astype(F32)
        for c in range(parts):
            rows_ref[c, e * PITCH : e * PITCH + RB, :] = piece[:, c * L : (c + 1) * L]
    for r in range(RB):
        d = [
            dot(
                st_ref[...],
                rows_ref[c, pl.ds(r, events, stride=PITCH), :].astype(BF),
            )
            for c in range(parts)
        ]
        for v in range(levels):
            turn_ref[v, r * transmits : (r + 1) * transmits, :] = (
                d[v + 1] - d[v]
            ) * 0.5
            dsum_ref[r : r + 1, v * L : (v + 1) * L] = (
                jnp.sum(d[v + 1] + d[v], axis=0, keepdims=True) * 0.5
            )
    for k in range(transmits):
        for v in range(levels):
            delta_ref[k, :, v * L : (v + 1) * L] = turn_ref[
                v, pl.ds(k, RB, stride=transmits), :
            ].astype(BF)


def decode(st, encoded):
    transmits, events = st.shape
    _, receivers, samples = encoded.shape
    diff = samples - L
    return pl.pallas_call(
        decode_kernel,
        grid=(receivers // RB,),
        in_specs=[
            pl.BlockSpec((transmits, events), lambda g: (0, 0)),
            pl.BlockSpec((events, RB, samples), lambda g: (0, g, 0)),
        ],
        out_specs=[
            pl.BlockSpec((transmits, RB, diff), lambda g: (0, g, 0)),
            pl.BlockSpec((RB, diff), lambda g: (g, 0)),
        ],
        out_shape=[
            jax.ShapeDtypeStruct((transmits, receivers, diff), BF),
            jax.ShapeDtypeStruct((receivers, diff), F32),
        ],
        scratch_shapes=[
            pltpu.VMEM((samples // L, events * PITCH, L), F32),
            pltpu.VMEM((diff // L, RB * transmits, L), F32),
        ],
        compiler_params=pltpu.CompilerParams(vmem_limit_bytes=50 * 2**20),
        cost_estimate=pl.CostEstimate(
            flops=16 * transmits * events * receivers * samples,
            bytes_accessed=events * receivers * samples * 2
            + transmits * receivers * diff * 2,
            transcendentals=0,
        ),
    )(st, encoded)


def beam_kernel(scale, mask_ref, delta_ref, dsum_ref, *refs):
    *tx_refs, out_ref, a_ref, s_ref, acc_ref, even_ref, odd_ref = refs
    block, receivers, diff = delta_ref.shape
    levels = diff // L
    half = block // 2
    groups, _, _, wide = mask_ref.shape
    step, last = pl.program_id(1), pl.num_programs(1) - 1

    def turn(x_to, side, k):
        for v in range(levels):
            x_to[k * L : (k + 1) * L, v * receivers : (v + 1) * receivers] = delta_ref[
                side * half + k, :, v * L : (v + 1) * L
            ].T

    def product(x_from, k0, beside):
        for g in range(groups):
            for k in range(g * half // groups, (g + 1) * half // groups):
                beside(k)
            here = slice(g * wide, (g + 1) * wide)
            y = dot(x_from[...], a_ref[:, here]).reshape(half, L // 8, 8, wide)
            acc = acc_ref[:, :, here]
            for k in range(half):
                acc = acc + s_ref[k0 + k, :, here] * y[k]
            acc_ref[:, :, here] = acc

    @pl.when(step == 0)
    def _():
        for v in range(levels):
            whole = dsum_ref[:, v * L : (v + 1) * L]
            high = whole.astype(BF)
            here = slice(v * receivers, (v + 1) * receivers)
            odd_ref[:L, here] = high.T
            odd_ref[L : 2 * L, here] = (whole - high.astype(F32)).astype(BF).T
        for g in range(groups):
            here = slice(g * wide, (g + 1) * wide)
            rx, on = mask_ref[g, 0].astype(F32), mask_ref[g, 1].astype(F32)
            for v in range(levels):
                a_ref[v * receivers : (v + 1) * receivers, here] = jnp.where(
                    rx == v, on, 0.0
                ).astype(BF)
            y = dot(odd_ref[: 2 * L, :], a_ref[:, here])
            acc_ref[:, :, here] = (y[:L] + y[L:]).reshape(L // 8, 8, wide)
            at = 0
            for ref in tx_refs:
                s = 2.0 * ref[:, here].astype(F32) - 1.0
                for k in range(ref.shape[0]):
                    s_ref[at + k, :, here] = jnp.broadcast_to(s[k : k + 1], (8, wide))
                at += ref.shape[0]
        for k in range(half):
            turn(even_ref, 0, k)

    @pl.when(step > 0)
    def _():
        product(odd_ref, step * block - half, functools.partial(turn, even_ref, 0))

    @pl.when(step < last)
    def _():
        product(even_ref, step * block, functools.partial(turn, odd_ref, 1))

    @pl.when(step == last)
    def _():
        stripes, _, deep, _ = out_ref.shape
        for g in range(groups):
            here = slice(g * wide, (g + 1) * wide)
            whole = (acc_ref[:, :, here] * scale).reshape(L, wide)
            for t in range(stripes):
                out_ref[t, g] = whole[t * deep : (t + 1) * deep, :].astype(BF)


def beamform(scale, stripes, masks, tx_bits, delta, dsum):
    groups, _, receivers, wide = masks.shape
    transmits, _, diff = delta.shape
    levels = diff // L
    block = 16
    some = min(groups, 8)
    steps = transmits // block
    return pl.pallas_call(
        functools.partial(beam_kernel, scale),
        grid=(groups // some, steps + 1),
        in_specs=[
            pl.BlockSpec((some, 2, receivers, wide), lambda p, k: (p, 0, 0, 0)),
            pl.BlockSpec(
                (block, receivers, diff), lambda p, k: (jnp.minimum(k, steps - 1), 0, 0)
            ),
            pl.BlockSpec((receivers, diff), lambda p, k: (0, 0)),
        ]
        + [
            pl.BlockSpec((t.shape[0], some * wide), lambda p, k: (0, p))
            for t in tx_bits
        ],
        out_specs=pl.BlockSpec(
            (stripes, some, L // stripes, wide), lambda p, k: (0, p, 0, 0)
        ),
        out_shape=jax.ShapeDtypeStruct((stripes, groups, L // stripes, wide), BF),
        scratch_shapes=[
            pltpu.VMEM((levels * receivers, some * wide), BF),
            pltpu.VMEM((transmits, 8, some * wide), F32),
            pltpu.VMEM((L // 8, 8, some * wide), F32),
            pltpu.VMEM((block // 2 * L, levels * receivers), BF),
            pltpu.VMEM((block // 2 * L, levels * receivers), BF),
        ],
        compiler_params=pltpu.CompilerParams(vmem_limit_bytes=50 * 2**20),
        cost_estimate=pl.CostEstimate(
            flops=2 * transmits * levels * receivers * groups * wide * L,
            bytes_accessed=transmits * receivers * diff * 2,
            transcendentals=0,
        ),
    )(masks, delta, dsum, *tx_bits)


def on_device(sizes, encoded, signs, tx_block, rx_block, apodization):
    lines_here = rx_block.shape[1]
    stripes, groups = sizes
    events, transmits = signs.shape
    receivers = rx_block.shape[0]
    at = lax.axis_index("tx").astype(jnp.int32).reshape(1)
    masks, own, st = cast(sizes, at, rx_block, apodization, tx_block, signs.T)
    masks = lax.all_to_all(masks, "img", 0, 0, tiled=True)
    tx_bits = [own] + [
        lax.ppermute(own, "tx", [((t + d) % stripes, t) for t in range(stripes)])
        for d in range(1, stripes)
    ]
    delta, dsum = decode(st, encoded)
    scale = math.sqrt(events / (transmits * receivers)) / events
    parts = beamform(scale, stripes, masks, tx_bits, delta, dsum)
    parts = parts.reshape(stripes * groups, L // stripes, lines_here)
    parts = lax.all_to_all(parts, ("tx", "img"), 0, 0, tiled=True)
    return jnp.sum(parts.astype(F32), axis=0).T


def solution(mesh):
    placed = (P("tx", "img", None), P(), P("tx", None), P(None, "img"), P(None, "img"))
    sizes = (mesh.shape["tx"], mesh.shape["img"])
    return jax.shard_map(
        functools.partial(on_device, sizes),
        mesh=mesh, in_specs=placed, out_specs=P("img", "tx"), check_vma=False,
    )
```

```python
import functools
import math

import jax
import jax.numpy as jnp
from jax import lax
from jax.experimental import pallas as pl
from jax.experimental.pallas import tpu as pltpu
from jax.sharding import PartitionSpec as P

L = 128
G = 8
RB = 16
BF = jnp.bfloat16
F32 = jnp.float32


def iota(shape, axis):
    return lax.broadcasted_iota(jnp.int32, shape, axis)


def dot(a, b):
    return jnp.dot(a, b, preferred_element_type=F32)


def cast_kernel(
    stripes, at_ref, rx_ref, on_ref, tx_ref, sign_ref, out_ref, bits_ref, st_ref
):
    out_ref[:, 0] = rx_ref[...].astype(F32).astype(BF)
    out_ref[:, 1] = on_ref[...].astype(F32).astype(BF)

    @pl.when(pl.program_id(0) == 0)
    def _():
        bits_ref[...] = tx_ref[...].astype(F32).astype(BF)
        every = st_ref.shape[0]
        turn = at_ref[0] * (every // stripes)
        row = lax.rem(iota((every, every), 0) + turn, every)
        up = (row == iota((every, every), 1)).astype(F32).astype(BF)
        st_ref[...] = dot(up, sign_ref[...].astype(F32).astype(BF)).astype(BF)


def cast(sizes, at, rx_block, apodization, tx_block, signs_t):
    stripes, groups = sizes
    receivers, lines_here = rx_block.shape
    every, events = signs_t.shape
    here = receivers // groups
    split = (groups, here, lines_here)
    whole = pl.BlockSpec(tx_block.shape, lambda i, at: (0, 0))
    part = pl.BlockSpec((groups // 2, here, lines_here), lambda i, at: (i, 0, 0))
    return pl.pallas_call(
        functools.partial(cast_kernel, stripes),
        grid_spec=pltpu.PrefetchScalarGridSpec(
            num_scalar_prefetch=1,
            grid=(2,),
            in_specs=[
                part,
                part,
                whole,
                pl.BlockSpec((every, events // stripes), lambda i, at: (0, at[0])),
            ],
            out_specs=[
                pl.BlockSpec(
                    (groups // 2, 2, here, lines_here), lambda i, at: (i, 0, 0, 0)
                ),
                whole,
                pl.BlockSpec((every, events // stripes), lambda i, at: (0, 0)),
            ],
        ),
        out_shape=[
            jax.ShapeDtypeStruct((groups, 2, here, lines_here), BF),
            jax.ShapeDtypeStruct(tx_block.shape, BF),
            jax.ShapeDtypeStruct((every, events // stripes), BF),
        ],
    )(at, rx_block.reshape(split), apodization.reshape(split), tx_block, signs_t)


def decode_kernel(st_ref, enc_ref, delta_ref, dsum_ref, sk_ref, low_ref, high_ref):
    transmits, events = st_ref.shape
    samples = enc_ref.shape[2]
    rows, depth = sk_ref.shape
    levels = samples // L - 1
    width = 32

    @pl.when(pl.program_id(0) == 0)
    def _():
        up = iota((rows, transmits), 0) // G == iota((rows, transmits), 1)
        tall = dot(up.astype(F32).astype(BF), st_ref[...]).astype(BF)
        wide = 512
        for at in range(0, depth, wide):
            out = (iota((events, wide), 1) + at) // G == iota((events, wide), 0)
            spread = dot(tall, out.astype(F32).astype(BF))
            same = iota((rows, wide), 0) % G == iota((rows, wide), 1) % G
            sk_ref[:, at : at + wide] = jnp.where(same, spread, 0.0).astype(BF)

    first = iota((1, RB, samples), 1) < G
    for at in range(0, events, width):
        piece = enc_ref[at : at + width].reshape(width // 2, 2, RB, samples)
        a, b = piece[:, 0], piece[:, 1]
        here = slice(at * G, (at + width) * G)
        low = jnp.where(first, a, pltpu.roll(b, G, 1))
        high = jnp.where(first, pltpu.roll(a, G, 1), b)
        low_ref[here, :] = low.reshape(width * G, samples)
        high_ref[here, :] = high.reshape(width * G, samples)
    deltas = []
    for half, x_ref in enumerate((low_ref, high_ref)):
        d = dot(sk_ref[...], x_ref[...])
        low, high = d[:, : samples - L], d[:, L:]
        deltas.append(((high - low) * 0.5).reshape(transmits, G, samples - L))
        mean = (high + low).reshape(transmits, G, samples - L)
        dsum_ref[half * G : (half + 1) * G, :] = jnp.sum(mean, axis=0) * 0.5
    delta_ref[...] = jnp.concatenate(deltas, axis=1).astype(BF)


def decode(st, encoded):
    transmits, events = st.shape
    _, receivers, samples = encoded.shape
    diff = samples - L
    return pl.pallas_call(
        decode_kernel,
        grid=(receivers // RB,),
        in_specs=[
            pl.BlockSpec((transmits, events), lambda g: (0, 0)),
            pl.BlockSpec((events, RB, samples), lambda g: (0, g, 0)),
        ],
        out_specs=[
            pl.BlockSpec((transmits, RB, diff), lambda g: (0, g, 0)),
            pl.BlockSpec((RB, diff), lambda g: (g, 0)),
        ],
        out_shape=[
            jax.ShapeDtypeStruct((transmits, receivers, diff), BF),
            jax.ShapeDtypeStruct((receivers, diff), F32),
        ],
        scratch_shapes=[
            pltpu.VMEM((transmits * G, events * G), BF),
            pltpu.VMEM((events * G, samples), BF),
            pltpu.VMEM((events * G, samples), BF),
        ],
        compiler_params=pltpu.CompilerParams(vmem_limit_bytes=50 * 2**20),
        cost_estimate=pl.CostEstimate(
            flops=16 * transmits * events * receivers * samples,
            bytes_accessed=events * receivers * samples * 2
            + transmits * receivers * diff * 2,
            transcendentals=0,
        ),
    )(st, encoded)


def beam_kernel(scale, mask_ref, delta_ref, dsum_ref, *refs):
    *tx_refs, out_ref, a_ref, s_ref, acc_ref, even_ref, odd_ref = refs
    block, receivers, diff = delta_ref.shape
    levels = diff // L
    half = block // 2
    groups, _, _, wide = mask_ref.shape
    step, last = pl.program_id(1), pl.num_programs(1) - 1

    def turn(x_to, side, k):
        for v in range(levels):
            x_to[k * L : (k + 1) * L, v * receivers : (v + 1) * receivers] = delta_ref[
                side * half + k, :, v * L : (v + 1) * L
            ].T

    def product(x_from, k0, beside):
        for g in range(groups):
            for k in range(g * half // groups, (g + 1) * half // groups):
                beside(k)
            here = slice(g * wide, (g + 1) * wide)
            y = dot(x_from[...], a_ref[:, here]).reshape(half, L // 8, 8, wide)
            acc = acc_ref[:, :, here]
            for k in range(half):
                acc = acc + s_ref[k0 + k, :, here] * y[k]
            acc_ref[:, :, here] = acc

    @pl.when(step == 0)
    def _():
        for v in range(levels):
            whole = dsum_ref[:, v * L : (v + 1) * L]
            high = whole.astype(BF)
            here = slice(v * receivers, (v + 1) * receivers)
            odd_ref[:L, here] = high.T
            odd_ref[L : 2 * L, here] = (whole - high.astype(F32)).astype(BF).T
        for g in range(groups):
            here = slice(g * wide, (g + 1) * wide)
            rx, on = mask_ref[g, 0].astype(F32), mask_ref[g, 1].astype(F32)
            for v in range(levels):
                a_ref[v * receivers : (v + 1) * receivers, here] = jnp.where(
                    rx == v, on, 0.0
                ).astype(BF)
            y = dot(odd_ref[: 2 * L, :], a_ref[:, here])
            acc_ref[:, :, here] = (y[:L] + y[L:]).reshape(L // 8, 8, wide)
            at = 0
            for ref in tx_refs:
                s = 2.0 * ref[:, here].astype(F32) - 1.0
                for k in range(ref.shape[0]):
                    s_ref[at + k, :, here] = jnp.broadcast_to(s[k : k + 1], (8, wide))
                at += ref.shape[0]
        for k in range(half):
            turn(even_ref, 0, k)

    @pl.when(step > 0)
    def _():
        product(odd_ref, step * block - half, functools.partial(turn, even_ref, 0))

    @pl.when(step < last)
    def _():
        product(even_ref, step * block, functools.partial(turn, odd_ref, 1))

    @pl.when(step == last)
    def _():
        stripes, _, deep, _ = out_ref.shape
        for g in range(groups):
            here = slice(g * wide, (g + 1) * wide)
            whole = (acc_ref[:, :, here] * scale).reshape(L, wide)
            for t in range(stripes):
                out_ref[t, g] = whole[t * deep : (t + 1) * deep, :].astype(BF)


def beamform(scale, stripes, masks, tx_bits, delta, dsum):
    groups, _, receivers, wide = masks.shape
    transmits, _, diff = delta.shape
    levels = diff // L
    block = min(32, transmits)
    some = min(groups, 8)
    steps = transmits // block
    return pl.pallas_call(
        functools.partial(beam_kernel, scale),
        grid=(groups // some, steps + 1),
        in_specs=[
            pl.BlockSpec((some, 2, receivers, wide), lambda p, k: (p, 0, 0, 0)),
            pl.BlockSpec(
                (block, receivers, diff), lambda p, k: (jnp.minimum(k, steps - 1), 0, 0)
            ),
            pl.BlockSpec((receivers, diff), lambda p, k: (0, 0)),
        ]
        + [
            pl.BlockSpec((t.shape[0], some * wide), lambda p, k: (0, p))
            for t in tx_bits
        ],
        out_specs=pl.BlockSpec(
            (stripes, some, L // stripes, wide), lambda p, k: (0, p, 0, 0)
        ),
        out_shape=jax.ShapeDtypeStruct((stripes, groups, L // stripes, wide), BF),
        scratch_shapes=[
            pltpu.VMEM((levels * receivers, some * wide), BF),
            pltpu.VMEM((transmits, 8, some * wide), F32),
            pltpu.VMEM((L // 8, 8, some * wide), F32),
            pltpu.VMEM((block // 2 * L, levels * receivers), BF),
            pltpu.VMEM((block // 2 * L, levels * receivers), BF),
        ],
        compiler_params=pltpu.CompilerParams(vmem_limit_bytes=50 * 2**20),
        cost_estimate=pl.CostEstimate(
            flops=2 * transmits * levels * receivers * groups * wide * L,
            bytes_accessed=transmits * receivers * diff * 2,
            transcendentals=0,
        ),
    )(masks, delta, dsum, *tx_bits)


def on_device(sizes, encoded, signs, tx_block, rx_block, apodization):
    lines_here = rx_block.shape[1]
    stripes, groups = sizes
    events, transmits = signs.shape
    receivers = rx_block.shape[0]
    at = lax.axis_index("tx").astype(jnp.int32).reshape(1)
    masks, own, st = cast(sizes, at, rx_block, apodization, tx_block, signs.T)
    masks = lax.all_to_all(masks, "img", 0, 0, tiled=True)
    tx_bits = [own] + [
        lax.ppermute(own, "tx", [((t + d) % stripes, t) for t in range(stripes)])
        for d in range(1, stripes)
    ]
    delta, dsum = decode(st, encoded)
    scale = math.sqrt(events / (transmits * receivers)) / events
    parts = beamform(scale, stripes, masks, tx_bits, delta, dsum)
    parts = parts.reshape(stripes * groups, L // stripes, lines_here)
    parts = lax.all_to_all(parts, ("tx", "img"), 0, 0, tiled=True)
    return jnp.sum(parts.astype(F32), axis=0).T


def solution(mesh):
    placed = (P("tx", "img", None), P(), P("tx", None), P(None, "img"), P(None, "img"))
    sizes = (mesh.shape["tx"], mesh.shape["img"])
    return jax.shard_map(
        functools.partial(on_device, sizes),
        mesh=mesh, in_specs=placed, out_specs=P("img", "tx"), check_vma=False,
    )
```

```python
import functools
import math

import jax
import jax.numpy as jnp
from jax import lax
from jax.experimental import pallas as pl
from jax.experimental.pallas import tpu as pltpu
from jax.sharding import PartitionSpec as P

L = 128
G = 4
RB = 16
BF = jnp.bfloat16
F32 = jnp.float32


def iota(shape, axis):
    return lax.broadcasted_iota(jnp.int32, shape, axis)


def dot(a, b):
    return jnp.dot(a, b, preferred_element_type=F32)


def cast_kernel(
    stripes, at_ref, rx_ref, on_ref, tx_ref, sign_ref, out_ref, bits_ref, st_ref
):
    out_ref[:, 0] = rx_ref[...].astype(F32).astype(BF)
    out_ref[:, 1] = on_ref[...].astype(F32).astype(BF)

    @pl.when(pl.program_id(0) == 0)
    def _():
        bits_ref[...] = tx_ref[...].astype(F32).astype(BF)
        every = st_ref.shape[0]
        turn = at_ref[0] * (every // stripes)
        row = lax.rem(iota((every, every), 0) + turn, every)
        up = (row == iota((every, every), 1)).astype(F32).astype(BF)
        st_ref[...] = dot(up, sign_ref[...].astype(F32).astype(BF)).astype(BF)


def cast(sizes, at, rx_block, apodization, tx_block, signs_t):
    stripes, groups = sizes
    receivers, lines_here = rx_block.shape
    every, events = signs_t.shape
    here = receivers // groups
    split = (groups, here, lines_here)
    whole = pl.BlockSpec(tx_block.shape, lambda i, at: (0, 0))
    part = pl.BlockSpec((groups // 2, here, lines_here), lambda i, at: (i, 0, 0))
    return pl.pallas_call(
        functools.partial(cast_kernel, stripes),
        grid_spec=pltpu.PrefetchScalarGridSpec(
            num_scalar_prefetch=1,
            grid=(2,),
            in_specs=[
                part,
                part,
                whole,
                pl.BlockSpec((every, events // stripes), lambda i, at: (0, at[0])),
            ],
            out_specs=[
                pl.BlockSpec(
                    (groups // 2, 2, here, lines_here), lambda i, at: (i, 0, 0, 0)
                ),
                whole,
                pl.BlockSpec((every, events // stripes), lambda i, at: (0, 0)),
            ],
        ),
        out_shape=[
            jax.ShapeDtypeStruct((groups, 2, here, lines_here), BF),
            jax.ShapeDtypeStruct(tx_block.shape, BF),
            jax.ShapeDtypeStruct((every, events // stripes), BF),
        ],
    )(at, rx_block.reshape(split), apodization.reshape(split), tx_block, signs_t)


def decode_kernel(st_ref, enc_ref, delta_ref, dsum_ref, sk_ref, x_ref):
    transmits, events = st_ref.shape
    samples = enc_ref.shape[2]
    rows, depth = sk_ref.shape
    diff = samples - L
    width = 32

    @pl.when(pl.program_id(0) == 0)
    def _():
        up = iota((rows, transmits), 0) // G == iota((rows, transmits), 1)
        tall = dot(up.astype(F32).astype(BF), st_ref[...]).astype(BF)
        wide = 256
        for at in range(0, depth, wide):
            row = iota((events, wide), 1) + at
            event = row // RB * 4 + row // G % 2 * 2 + row // (2 * G) % 2
            out = event == iota((events, wide), 0)
            spread = dot(tall, out.astype(F32).astype(BF))
            same = iota((rows, wide), 0) % G == iota((rows, wide), 1) % G
            sk_ref[:, at : at + wide] = jnp.where(same, spread, 0.0).astype(BF)

    row = iota((1, RB, samples), 1)
    first, inner = row < 2 * G, row % (2 * G) < G
    for at in range(0, events, width):
        piece = enc_ref[at : at + width].reshape(width // 4, 4, RB, samples)
        a, b, c, d = (piece[:, e] for e in range(4))
        here = slice(at * G, (at + width) * G)
        for side in range(2):
            if side == 0:
                ab = jnp.where(first, a, pltpu.roll(b, 2 * G, 1))
                cd = jnp.where(first, c, pltpu.roll(d, 2 * G, 1))
            else:
                ab = jnp.where(first, pltpu.roll(a, 2 * G, 1), b)
                cd = jnp.where(first, pltpu.roll(c, 2 * G, 1), d)
            low = jnp.where(inner, ab, pltpu.roll(cd, G, 1))
            high = jnp.where(inner, pltpu.roll(ab, RB - G, 1), cd)
            x_ref[2 * side, here, :] = low.reshape(width * G, samples)
            x_ref[2 * side + 1, here, :] = high.reshape(width * G, samples)
    deltas = []
    for q in range(RB // G):
        d = dot(sk_ref[...], x_ref[q])
        low, high = d[:, :diff], d[:, L:]
        deltas.append(((high - low) * 0.5).reshape(transmits // 2, 2 * G, diff))
        mean = jnp.sum((high + low).reshape(transmits // 2, 2 * G, diff), axis=0)
        dsum_ref[q * G : (q + 1) * G, :] = (mean[:G] + mean[G:]) * 0.5
    upper = iota((1, 2 * G, diff), 1) < G
    evens, odds = [], []
    for side in range(2):
        low, high = deltas[2 * side], deltas[2 * side + 1]
        evens.append(jnp.where(upper, low, pltpu.roll(high, G, 1)))
        odds.append(jnp.where(upper, pltpu.roll(low, G, 1), high))
    delta_ref[:, 0] = jnp.concatenate(evens, axis=1).astype(BF)
    delta_ref[:, 1] = jnp.concatenate(odds, axis=1).astype(BF)


def decode(st, encoded):
    transmits, events = st.shape
    _, receivers, samples = encoded.shape
    diff = samples - L
    return pl.pallas_call(
        decode_kernel,
        grid=(receivers // RB,),
        in_specs=[
            pl.BlockSpec((transmits, events), lambda g: (0, 0)),
            pl.BlockSpec((events, RB, samples), lambda g: (0, g, 0)),
        ],
        out_specs=[
            pl.BlockSpec((transmits // 2, 2, RB, diff), lambda g: (0, 0, g, 0)),
            pl.BlockSpec((RB, diff), lambda g: (g, 0)),
        ],
        out_shape=[
            jax.ShapeDtypeStruct((transmits // 2, 2, receivers, diff), BF),
            jax.ShapeDtypeStruct((receivers, diff), F32),
        ],
        scratch_shapes=[
            pltpu.VMEM((transmits * G, events * G), BF),
            pltpu.VMEM((RB // G, events * G, samples), BF),
        ],
        compiler_params=pltpu.CompilerParams(vmem_limit_bytes=50 * 2**20),
        cost_estimate=pl.CostEstimate(
            flops=16 * transmits * events * receivers * samples,
            bytes_accessed=events * receivers * samples * 2
            + transmits * receivers * diff * 2,
            transcendentals=0,
        ),
    )(st, encoded)


def beam_kernel(scale, mask_ref, delta_ref, dsum_ref, *refs):
    *tx_refs, out_ref, a_ref, s_ref, acc_ref, even_ref, odd_ref = refs
    block, receivers, diff = delta_ref.shape
    levels = diff // L
    half = block // 2
    groups, _, _, wide = mask_ref.shape
    step, last = pl.program_id(1), pl.num_programs(1) - 1

    def turn(x_to, side, k):
        for v in range(levels):
            x_to[k * L : (k + 1) * L, v * receivers : (v + 1) * receivers] = delta_ref[
                side * half + k, :, v * L : (v + 1) * L
            ].T

    def product(x_from, k0, beside):
        for g in range(groups):
            for k in range(g * half // groups, (g + 1) * half // groups):
                beside(k)
            here = slice(g * wide, (g + 1) * wide)
            y = dot(x_from[...], a_ref[:, here]).reshape(half, L // 8, 8, wide)
            acc = acc_ref[:, :, here]
            for k in range(half):
                acc = acc + s_ref[k0 + k, :, here] * y[k]
            acc_ref[:, :, here] = acc

    @pl.when(step == 0)
    def _():
        for v in range(levels):
            whole = dsum_ref[:, v * L : (v + 1) * L]
            high = whole.astype(BF)
            here = slice(v * receivers, (v + 1) * receivers)
            odd_ref[:L, here] = high.T
            odd_ref[L : 2 * L, here] = (whole - high.astype(F32)).astype(BF).T
        for g in range(groups):
            here = slice(g * wide, (g + 1) * wide)
            rx, on = mask_ref[g, 0].astype(F32), mask_ref[g, 1].astype(F32)
            for v in range(levels):
                a_ref[v * receivers : (v + 1) * receivers, here] = jnp.where(
                    rx == v, on, 0.0
                ).astype(BF)
            y = dot(odd_ref[: 2 * L, :], a_ref[:, here])
            acc_ref[:, :, here] = (y[:L] + y[L:]).reshape(L // 8, 8, wide)
            at = 0
            for ref in tx_refs:
                s = 2.0 * ref[:, here].astype(F32) - 1.0
                for k in range(ref.shape[0]):
                    s_ref[at + k, :, here] = jnp.broadcast_to(s[k : k + 1], (8, wide))
                at += ref.shape[0]
        for k in range(half):
            turn(even_ref, 0, k)

    @pl.when(step > 0)
    def _():
        product(odd_ref, step * block - half, functools.partial(turn, even_ref, 0))

    @pl.when(step < last)
    def _():
        product(even_ref, step * block, functools.partial(turn, odd_ref, 1))

    @pl.when(step == last)
    def _():
        stripes, _, deep, _ = out_ref.shape
        for g in range(groups):
            here = slice(g * wide, (g + 1) * wide)
            whole = (acc_ref[:, :, here] * scale).reshape(L, wide)
            for t in range(stripes):
                out_ref[t, g] = whole[t * deep : (t + 1) * deep, :].astype(BF)


def beamform(scale, stripes, masks, tx_bits, delta, dsum):
    groups, _, receivers, wide = masks.shape
    transmits, _, diff = delta.shape
    levels = diff // L
    block = min(16, transmits)
    some = min(groups, 8)
    steps = transmits // block
    return pl.pallas_call(
        functools.partial(beam_kernel, scale),
        grid=(groups // some, steps + 1),
        in_specs=[
            pl.BlockSpec((some, 2, receivers, wide), lambda p, k: (p, 0, 0, 0)),
            pl.BlockSpec(
                (block, receivers, diff), lambda p, k: (jnp.minimum(k, steps - 1), 0, 0)
            ),
            pl.BlockSpec((receivers, diff), lambda p, k: (0, 0)),
        ]
        + [
            pl.BlockSpec((t.shape[0], some * wide), lambda p, k: (0, p))
            for t in tx_bits
        ],
        out_specs=pl.BlockSpec(
            (stripes, some, L // stripes, wide), lambda p, k: (0, p, 0, 0)
        ),
        out_shape=jax.ShapeDtypeStruct((stripes, groups, L // stripes, wide), BF),
        scratch_shapes=[
            pltpu.VMEM((levels * receivers, some * wide), BF),
            pltpu.VMEM((transmits, 8, some * wide), F32),
            pltpu.VMEM((L // 8, 8, some * wide), F32),
            pltpu.VMEM((block // 2 * L, levels * receivers), BF),
            pltpu.VMEM((block // 2 * L, levels * receivers), BF),
        ],
        compiler_params=pltpu.CompilerParams(vmem_limit_bytes=50 * 2**20),
        cost_estimate=pl.CostEstimate(
            flops=2 * transmits * levels * receivers * groups * wide * L,
            bytes_accessed=transmits * receivers * diff * 2,
            transcendentals=0,
        ),
    )(masks, delta, dsum, *tx_bits)


def on_device(sizes, encoded, signs, tx_block, rx_block, apodization):
    lines_here = rx_block.shape[1]
    stripes, groups = sizes
    events, transmits = signs.shape
    receivers = rx_block.shape[0]
    at = lax.axis_index("tx").astype(jnp.int32).reshape(1)
    masks, own, st = cast(sizes, at, rx_block, apodization, tx_block, signs.T)
    masks = lax.all_to_all(masks, "img", 0, 0, tiled=True)
    tx_bits = [own] + [
        lax.ppermute(own, "tx", [((t + d) % stripes, t) for t in range(stripes)])
        for d in range(1, stripes)
    ]
    delta, dsum = decode(st, encoded)
    delta = delta.reshape(transmits, *delta.shape[2:])
    scale = math.sqrt(events / (transmits * receivers)) / events
    parts = beamform(scale, stripes, masks, tx_bits, delta, dsum)
    parts = parts.reshape(stripes * groups, L // stripes, lines_here)
    parts = lax.all_to_all(parts, ("tx", "img"), 0, 0, tiled=True)
    return jnp.sum(parts.astype(F32), axis=0).T


def solution(mesh):
    placed = (P("tx", "img", None), P(), P("tx", None), P(None, "img"), P(None, "img"))
    sizes = (mesh.shape["tx"], mesh.shape["img"])
    return jax.shard_map(
        functools.partial(on_device, sizes),
        mesh=mesh, in_specs=placed, out_specs=P("img", "tx"), check_vma=False,
    )
```

```python
import functools
import math

import jax
import jax.numpy as jnp
from jax import lax
from jax.experimental import pallas as pl
from jax.experimental.pallas import tpu as pltpu
from jax.sharding import PartitionSpec as P

L = 128
G = 4
RB = 16
BF = jnp.bfloat16
F32 = jnp.float32


def iota(shape, axis):
    return lax.broadcasted_iota(jnp.int32, shape, axis)


def dot(a, b):
    return jnp.dot(a, b, preferred_element_type=F32)


def cast_kernel(
    stripes, at_ref, rx_ref, on_ref, sign_ref, out_ref, st_ref
):
    out_ref[:, 0] = rx_ref[...].astype(F32).astype(BF)
    out_ref[:, 1] = on_ref[...].astype(F32).astype(BF)

    @pl.when(pl.program_id(0) == 0)
    def _():
        every = st_ref.shape[0]
        turn = at_ref[0] * (every // stripes)
        row = lax.rem(iota((every, every), 0) + turn, every)
        up = (row == iota((every, every), 1)).astype(F32).astype(BF)
        st_ref[...] = dot(up, sign_ref[...].astype(F32).astype(BF)).astype(BF)


def cast(sizes, at, rx_block, apodization, signs_t):
    stripes, groups = sizes
    receivers, lines_here = rx_block.shape
    every, events = signs_t.shape
    here = receivers // groups
    split = (groups, here, lines_here)
    part = pl.BlockSpec((groups // 2, here, lines_here), lambda i, at: (i, 0, 0))
    return pl.pallas_call(
        functools.partial(cast_kernel, stripes),
        grid_spec=pltpu.PrefetchScalarGridSpec(
            num_scalar_prefetch=1,
            grid=(2,),
            in_specs=[
                part,
                part,
                pl.BlockSpec((every, events // stripes), lambda i, at: (0, at[0])),
            ],
            out_specs=[
                pl.BlockSpec(
                    (groups // 2, 2, here, lines_here), lambda i, at: (i, 0, 0, 0)
                ),
                pl.BlockSpec((every, events // stripes), lambda i, at: (0, 0)),
            ],
        ),
        out_shape=[
            jax.ShapeDtypeStruct((groups, 2, here, lines_here), BF),
            jax.ShapeDtypeStruct((every, events // stripes), BF),
        ],
    )(at, rx_block.reshape(split), apodization.reshape(split), signs_t)


def decode_kernel(st_ref, enc_ref, delta_ref, dsum_ref, sk_ref, x_ref):
    transmits, events = st_ref.shape
    samples = enc_ref.shape[2]
    _, rows, depth = sk_ref.shape
    diff = samples - L
    width = 32

    @pl.when(pl.program_id(0) == 0)
    def _():
        k = iota((rows, transmits), 0) // G
        talls = []
        for swap in (k, k + 1 - 2 * (k % 2)):
            up = (swap == iota((rows, transmits), 1)).astype(F32).astype(BF)
            talls.append(dot(up, st_ref[...]).astype(BF))
        wide = 256
        for at in range(0, depth, wide):
            row = iota((events, wide), 1) + at
            event = row // RB * 4 + row // G % 2 * 2 + row // (2 * G) % 2
            out = event == iota((events, wide), 0)
            out = out.astype(F32).astype(BF)
            same = iota((rows, wide), 0) % G == iota((rows, wide), 1) % G
            for side, tall in enumerate(talls):
                spread = jnp.where(same, dot(tall, out), 0.0)
                sk_ref[side, :, at : at + wide] = spread.astype(BF)

    row = iota((1, RB, samples), 1)
    first, inner = row < 2 * G, row % (2 * G) < G
    for at in range(0, events, width):
        piece = enc_ref[at : at + width].reshape(width // 4, 4, RB, samples)
        a, b, c, d = (piece[:, e] for e in range(4))
        here = slice(at * G, (at + width) * G)
        for side in range(2):
            if side == 0:
                ab = jnp.where(first, a, pltpu.roll(b, 2 * G, 1))
                cd = jnp.where(first, c, pltpu.roll(d, 2 * G, 1))
            else:
                ab = jnp.where(first, pltpu.roll(a, 2 * G, 1), b)
                cd = jnp.where(first, pltpu.roll(c, 2 * G, 1), d)
            low = jnp.where(inner, ab, pltpu.roll(cd, G, 1))
            high = jnp.where(inner, pltpu.roll(ab, RB - G, 1), cd)
            x_ref[2 * side, here, :] = low.reshape(width * G, samples)
            x_ref[2 * side + 1, here, :] = high.reshape(width * G, samples)
    deltas = []
    for q in range(RB // G):
        d = dot(sk_ref[q % 2], x_ref[q])
        low, high = d[:, :diff], d[:, L:]
        deltas.append(((high - low) * 0.5).reshape(transmits // 2, 2 * G, diff))
        mean = jnp.sum((high + low).reshape(transmits // 2, 2 * G, diff), axis=0)
        dsum_ref[q * G : (q + 1) * G, :] = (mean[:G] + mean[G:]) * 0.5
    upper = iota((1, 2 * G, diff), 1) < G
    evens, odds = [], []
    for side in range(2):
        low, high = deltas[2 * side], deltas[2 * side + 1]
        evens.append(jnp.where(upper, low, high))
        odds.append(jnp.where(upper, high, low))
    delta_ref[:, 0] = jnp.concatenate(evens, axis=1).astype(BF)
    swapped = jnp.concatenate(odds, axis=1).astype(BF)
    inner = iota((1, RB, diff), 1) % (2 * G) < G
    delta_ref[:, 1] = jnp.where(
        inner, pltpu.roll(swapped, RB - G, 1), pltpu.roll(swapped, G, 1)
    )


def decode(st, encoded):
    transmits, events = st.shape
    _, receivers, samples = encoded.shape
    diff = samples - L
    return pl.pallas_call(
        decode_kernel,
        grid=(receivers // RB,),
        in_specs=[
            pl.BlockSpec((transmits, events), lambda g: (0, 0)),
            pl.BlockSpec((events, RB, samples), lambda g: (0, g, 0)),
        ],
        out_specs=[
            pl.BlockSpec((transmits // 2, 2, RB, diff), lambda g: (0, 0, g, 0)),
            pl.BlockSpec((RB, diff), lambda g: (g, 0)),
        ],
        out_shape=[
            jax.ShapeDtypeStruct((transmits // 2, 2, receivers, diff), BF),
            jax.ShapeDtypeStruct((receivers, diff), F32),
        ],
        scratch_shapes=[
            pltpu.VMEM((2, transmits * G, events * G), BF),
            pltpu.VMEM((RB // G, events * G, samples), BF),
        ],
        compiler_params=pltpu.CompilerParams(vmem_limit_bytes=50 * 2**20),
        cost_estimate=pl.CostEstimate(
            flops=16 * transmits * events * receivers * samples,
            bytes_accessed=events * receivers * samples * 2
            + transmits * receivers * diff * 2,
            transcendentals=0,
        ),
    )(st, encoded)


def beam_kernel(scale, mask_ref, delta_ref, dsum_ref, *refs):
    *tx_refs, out_ref, a_ref, s_ref, acc_ref, even_ref, odd_ref = refs
    block, receivers, diff = delta_ref.shape
    levels = diff // L
    half = block // 2
    groups, _, _, wide = mask_ref.shape
    step, last = pl.program_id(1), pl.num_programs(1) - 1

    def turn(x_to, side, k):
        for v in range(levels):
            x_to[k * L : (k + 1) * L, v * receivers : (v + 1) * receivers] = delta_ref[
                side * half + k, :, v * L : (v + 1) * L
            ].T

    def product(x_from, k0, beside):
        for g in range(groups):
            for k in range(g * half // groups, (g + 1) * half // groups):
                beside(k)
            here = slice(g * wide, (g + 1) * wide)
            y = dot(x_from[...], a_ref[:, here]).reshape(half, L // 8, 8, wide)
            acc = acc_ref[:, :, here]
            for k in range(half):
                acc = acc + s_ref[k0 + k, :, here] * y[k]
            acc_ref[:, :, here] = acc

    @pl.when(step == 0)
    def _():
        for v in range(levels):
            whole = dsum_ref[:, v * L : (v + 1) * L]
            high = whole.astype(BF)
            here = slice(v * receivers, (v + 1) * receivers)
            odd_ref[:L, here] = high.T
            odd_ref[L : 2 * L, here] = (whole - high.astype(F32)).astype(BF).T
        for g in range(groups):
            here = slice(g * wide, (g + 1) * wide)
            rx, on = mask_ref[g, 0].astype(F32), mask_ref[g, 1].astype(F32)
            for v in range(levels):
                a_ref[v * receivers : (v + 1) * receivers, here] = jnp.where(
                    rx == v, on, 0.0
                ).astype(BF)
            y = dot(odd_ref[: 2 * L, :], a_ref[:, here])
            acc_ref[:, :, here] = (y[:L] + y[L:]).reshape(L // 8, 8, wide)
            at = 0
            for ref in tx_refs:
                s = 2.0 * ref[:, here].astype(F32) - 1.0
                for k in range(ref.shape[0]):
                    s_ref[at + k, :, here] = jnp.broadcast_to(s[k : k + 1], (8, wide))
                at += ref.shape[0]
        for k in range(half):
            turn(even_ref, 0, k)

    @pl.when(step > 0)
    def _():
        product(odd_ref, step * block - half, functools.partial(turn, even_ref, 0))

    @pl.when(step < last)
    def _():
        product(even_ref, step * block, functools.partial(turn, odd_ref, 1))

    @pl.when(step == last)
    def _():
        stripes, _, deep, _ = out_ref.shape
        for g in range(groups):
            here = slice(g * wide, (g + 1) * wide)
            whole = (acc_ref[:, :, here] * scale).reshape(L, wide)
            for t in range(stripes):
                out_ref[t, g] = whole[t * deep : (t + 1) * deep, :].astype(BF)


def beamform(scale, stripes, masks, tx_bits, delta, dsum):
    groups, _, receivers, wide = masks.shape
    transmits, _, diff = delta.shape
    levels = diff // L
    block = min(16, transmits)
    some = min(groups, 8)
    steps = transmits // block
    return pl.pallas_call(
        functools.partial(beam_kernel, scale),
        grid=(groups // some, steps + 1),
        in_specs=[
            pl.BlockSpec((some, 2, receivers, wide), lambda p, k: (p, 0, 0, 0)),
            pl.BlockSpec(
                (block, receivers, diff), lambda p, k: (jnp.minimum(k, steps - 1), 0, 0)
            ),
            pl.BlockSpec((receivers, diff), lambda p, k: (0, 0)),
        ]
        + [
            pl.BlockSpec((t.shape[0], some * wide), lambda p, k: (0, p))
            for t in tx_bits
        ],
        out_specs=pl.BlockSpec(
            (stripes, some, L // stripes, wide), lambda p, k: (0, p, 0, 0)
        ),
        out_shape=jax.ShapeDtypeStruct((stripes, groups, L // stripes, wide), BF),
        scratch_shapes=[
            pltpu.VMEM((levels * receivers, some * wide), BF),
            pltpu.VMEM((transmits, 8, some * wide), F32),
            pltpu.VMEM((L // 8, 8, some * wide), F32),
            pltpu.VMEM((block // 2 * L, levels * receivers), BF),
            pltpu.VMEM((block // 2 * L, levels * receivers), BF),
        ],
        compiler_params=pltpu.CompilerParams(vmem_limit_bytes=50 * 2**20),
        cost_estimate=pl.CostEstimate(
            flops=2 * transmits * levels * receivers * groups * wide * L,
            bytes_accessed=transmits * receivers * diff * 2,
            transcendentals=0,
        ),
    )(masks, delta, dsum, *tx_bits)


def on_device(sizes, encoded, signs, tx_block, rx_block, apodization):
    lines_here = rx_block.shape[1]
    stripes, groups = sizes
    events, transmits = signs.shape
    receivers = rx_block.shape[0]
    at = lax.axis_index("tx").astype(jnp.int32).reshape(1)
    masks, st = cast(sizes, at, rx_block, apodization, signs.T)
    masks = lax.all_to_all(masks, "img", 0, 0, tiled=True)
    tx_bits = [tx_block] + [
        lax.ppermute(tx_block, "tx", [((t + d) % stripes, t) for t in range(stripes)])
        for d in range(1, stripes)
    ]
    delta, dsum = decode(st, encoded)
    delta = delta.reshape(transmits, *delta.shape[2:])
    scale = math.sqrt(events / (transmits * receivers)) / events
    parts = beamform(scale, stripes, masks, tx_bits, delta, dsum)
    parts = parts.reshape(stripes * groups, L // stripes, lines_here)
    parts = lax.all_to_all(parts, ("tx", "img"), 0, 0, tiled=True)
    return jnp.sum(parts.astype(F32), axis=0).T


def solution(mesh):
    placed = (P("tx", "img", None), P(), P("tx", None), P(None, "img"), P(None, "img"))
    sizes = (mesh.shape["tx"], mesh.shape["img"])
    return jax.shard_map(
        functools.partial(on_device, sizes),
        mesh=mesh, in_specs=placed, out_specs=P("img", "tx"), check_vma=False,
    )
```

```python
import functools
import math

import jax
import jax.numpy as jnp
from jax import lax
from jax.experimental import pallas as pl
from jax.experimental.pallas import tpu as pltpu
from jax.sharding import PartitionSpec as P

L = 128
G = 4
RB = 16
BF = jnp.bfloat16
F32 = jnp.float32


def iota(shape, axis):
    return lax.broadcasted_iota(jnp.int32, shape, axis)


def dot(a, b):
    return jnp.dot(a, b, preferred_element_type=F32)


def cast_kernel(
    stripes, at_ref, rx_ref, on_ref, tx_ref, sign_ref, out_ref, bits_ref, st_ref
):
    out_ref[:, 0] = rx_ref[...].astype(F32).astype(BF)
    out_ref[:, 1] = on_ref[...].astype(F32).astype(BF)

    @pl.when(pl.program_id(0) == 0)
    def _():
        bits_ref[...] = tx_ref[...].astype(F32).astype(BF)
        every = st_ref.shape[0]
        turn = at_ref[0] * (every // stripes)
        row = lax.rem(iota((every, every), 0) + turn, every)
        up = (row == iota((every, every), 1)).astype(F32).astype(BF)
        st_ref[...] = dot(up, sign_ref[...].astype(F32).astype(BF)).astype(BF)


def cast(sizes, at, rx_block, apodization, tx_block, signs_t):
    stripes, groups = sizes
    receivers, lines_here = rx_block.shape
    every, events = signs_t.shape
    here = receivers // groups
    split = (groups, here, lines_here)
    whole = pl.BlockSpec(tx_block.shape, lambda i, at: (0, 0))
    part = pl.BlockSpec((groups // 2, here, lines_here), lambda i, at: (i, 0, 0))
    return pl.pallas_call(
        functools.partial(cast_kernel, stripes),
        grid_spec=pltpu.PrefetchScalarGridSpec(
            num_scalar_prefetch=1,
            grid=(2,),
            in_specs=[
                part,
                part,
                whole,
                pl.BlockSpec((every, events // stripes), lambda i, at: (0, at[0])),
            ],
            out_specs=[
                pl.BlockSpec(
                    (groups // 2, 2, here, lines_here), lambda i, at: (i, 0, 0, 0)
                ),
                whole,
                pl.BlockSpec((every, events // stripes), lambda i, at: (0, 0)),
            ],
        ),
        out_shape=[
            jax.ShapeDtypeStruct((groups, 2, here, lines_here), BF),
            jax.ShapeDtypeStruct(tx_block.shape, BF),
            jax.ShapeDtypeStruct((every, events // stripes), BF),
        ],
    )(at, rx_block.reshape(split), apodization.reshape(split), tx_block, signs_t)


def decode_kernel(
    st_ref, enc_ref, delta_ref, dsum_ref, sk_ref, lower_ref, upper_ref
):
    transmits, events = st_ref.shape
    samples = enc_ref.shape[2]
    rows, depth = sk_ref.shape
    diff = samples - L
    width = 32

    @pl.when(pl.program_id(0) == 0)
    def _():
        up = iota((rows, transmits), 0) // G == iota((rows, transmits), 1)
        tall = dot(up.astype(F32).astype(BF), st_ref[...]).astype(BF)
        wide = 256
        for at in range(0, depth, wide):
            row = iota((events, wide), 1) + at
            event = row // RB * 4 + row // G % 2 * 2 + row // (2 * G) % 2
            out = event == iota((events, wide), 0)
            spread = dot(tall, out.astype(F32).astype(BF))
            same = iota((rows, wide), 0) % G == iota((rows, wide), 1) % G
            sk_ref[:, at : at + wide] = jnp.where(same, spread, 0.0).astype(BF)

    row = iota((1, RB, samples), 1)
    first, inner = row < 2 * G, row % (2 * G) < G

    def lay_out(x_ref, side, at):
        piece = enc_ref[at : at + width].reshape(width // 4, 4, RB, samples)
        a, b, c, d = (piece[:, e] for e in range(4))
        here = slice(at * G, (at + width) * G)
        if side == 0:
            ab = jnp.where(first, a, pltpu.roll(b, 2 * G, 1))
            cd = jnp.where(first, c, pltpu.roll(d, 2 * G, 1))
        else:
            ab = jnp.where(first, pltpu.roll(a, 2 * G, 1), b)
            cd = jnp.where(first, pltpu.roll(c, 2 * G, 1), d)
        low = jnp.where(inner, ab, pltpu.roll(cd, G, 1))
        high = jnp.where(inner, pltpu.roll(ab, RB - G, 1), cd)
        x_ref[0, here, :] = low.reshape(width * G, samples)
        x_ref[1, here, :] = high.reshape(width * G, samples)

    deltas = []

    def product(q, x):
        d = dot(sk_ref[...], x)
        low, high = d[:, :diff], d[:, L:]
        deltas.append(((high - low) * 0.5).reshape(transmits // 2, 2 * G, diff))
        mean = jnp.sum((high + low).reshape(transmits // 2, 2 * G, diff), axis=0)
        dsum_ref[q * G : (q + 1) * G, :] = (mean[:G] + mean[G:]) * 0.5

    for at in range(0, events, width):
        lay_out(lower_ref, 0, at)
    for q in range(2):
        for at in range(q * events // 2, (q + 1) * events // 2, width):
            lay_out(upper_ref, 1, at)
        product(q, lower_ref[q])
    for q in range(2):
        product(2 + q, upper_ref[q])
    upper = iota((1, 2 * G, diff), 1) < G
    evens, odds = [], []
    for side in range(2):
        low, high = deltas[2 * side], deltas[2 * side + 1]
        evens.append(jnp.where(upper, low, pltpu.roll(high, G, 1)))
        odds.append(jnp.where(upper, pltpu.roll(low, G, 1), high))
    delta_ref[:, 0] = jnp.concatenate(evens, axis=1).astype(BF)
    delta_ref[:, 1] = jnp.concatenate(odds, axis=1).astype(BF)


def decode(st, encoded):
    transmits, events = st.shape
    _, receivers, samples = encoded.shape
    diff = samples - L
    return pl.pallas_call(
        decode_kernel,
        grid=(receivers // RB,),
        in_specs=[
            pl.BlockSpec((transmits, events), lambda g: (0, 0)),
            pl.BlockSpec((events, RB, samples), lambda g: (0, g, 0)),
        ],
        out_specs=[
            pl.BlockSpec((transmits // 2, 2, RB, diff), lambda g: (0, 0, g, 0)),
            pl.BlockSpec((RB, diff), lambda g: (g, 0)),
        ],
        out_shape=[
            jax.ShapeDtypeStruct((transmits // 2, 2, receivers, diff), BF),
            jax.ShapeDtypeStruct((receivers, diff), F32),
        ],
        scratch_shapes=[
            pltpu.VMEM((transmits * G, events * G), BF),
            pltpu.VMEM((2, events * G, samples), BF),
            pltpu.VMEM((2, events * G, samples), BF),
        ],
        compiler_params=pltpu.CompilerParams(vmem_limit_bytes=50 * 2**20),
        cost_estimate=pl.CostEstimate(
            flops=16 * transmits * events * receivers * samples,
            bytes_accessed=events * receivers * samples * 2
            + transmits * receivers * diff * 2,
            transcendentals=0,
        ),
    )(st, encoded)


def beam_kernel(scale, mask_ref, delta_ref, dsum_ref, *refs):
    *tx_refs, out_ref, a_ref, s_ref, acc_ref, even_ref, odd_ref = refs
    block, receivers, diff = delta_ref.shape
    levels = diff // L
    half = block // 2
    groups, _, _, wide = mask_ref.shape
    step, last = pl.program_id(1), pl.num_programs(1) - 1

    def turn(x_to, side, k):
        for v in range(levels):
            x_to[k * L : (k + 1) * L, v * receivers : (v + 1) * receivers] = delta_ref[
                side * half + k, :, v * L : (v + 1) * L
            ].T

    def product(x_from, k0, beside):
        for g in range(groups):
            for k in range(g * half // groups, (g + 1) * half // groups):
                beside(k)
            here = slice(g * wide, (g + 1) * wide)
            y = dot(x_from[...], a_ref[:, here]).reshape(half, L // 8, 8, wide)
            acc = acc_ref[:, :, here]
            for k in range(half):
                acc = acc + s_ref[k0 + k, :, here] * y[k]
            acc_ref[:, :, here] = acc

    @pl.when(step == 0)
    def _():
        for v in range(levels):
            whole = dsum_ref[:, v * L : (v + 1) * L]
            high = whole.astype(BF)
            here = slice(v * receivers, (v + 1) * receivers)
            odd_ref[:L, here] = high.T
            odd_ref[L : 2 * L, here] = (whole - high.astype(F32)).astype(BF).T
        for g in range(groups):
            here = slice(g * wide, (g + 1) * wide)
            rx, on = mask_ref[g, 0].astype(F32), mask_ref[g, 1].astype(F32)
            for v in range(levels):
                a_ref[v * receivers : (v + 1) * receivers, here] = jnp.where(
                    rx == v, on, 0.0
                ).astype(BF)
            y = dot(odd_ref[: 2 * L, :], a_ref[:, here])
            acc_ref[:, :, here] = (y[:L] + y[L:]).reshape(L // 8, 8, wide)
            at = 0
            for ref in tx_refs:
                s = 2.0 * ref[:, here].astype(F32) - 1.0
                for k in range(ref.shape[0]):
                    s_ref[at + k, :, here] = jnp.broadcast_to(s[k : k + 1], (8, wide))
                at += ref.shape[0]
        for k in range(half):
            turn(even_ref, 0, k)

    @pl.when(step > 0)
    def _():
        product(odd_ref, step * block - half, functools.partial(turn, even_ref, 0))

    @pl.when(step < last)
    def _():
        product(even_ref, step * block, functools.partial(turn, odd_ref, 1))

    @pl.when(step == last)
    def _():
        stripes, _, deep, _ = out_ref.shape
        for g in range(groups):
            here = slice(g * wide, (g + 1) * wide)
            whole = (acc_ref[:, :, here] * scale).reshape(L, wide)
            for t in range(stripes):
                out_ref[t, g] = whole[t * deep : (t + 1) * deep, :].astype(BF)


def beamform(scale, stripes, masks, tx_bits, delta, dsum):
    groups, _, receivers, wide = masks.shape
    transmits, _, diff = delta.shape
    levels = diff // L
    block = min(16, transmits)
    some = min(groups, 8)
    steps = transmits // block
    return pl.pallas_call(
        functools.partial(beam_kernel, scale),
        grid=(groups // some, steps + 1),
        in_specs=[
            pl.BlockSpec((some, 2, receivers, wide), lambda p, k: (p, 0, 0, 0)),
            pl.BlockSpec(
                (block, receivers, diff), lambda p, k: (jnp.minimum(k, steps - 1), 0, 0)
            ),
            pl.BlockSpec((receivers, diff), lambda p, k: (0, 0)),
        ]
        + [
            pl.BlockSpec((t.shape[0], some * wide), lambda p, k: (0, p))
            for t in tx_bits
        ],
        out_specs=pl.BlockSpec(
            (stripes, some, L // stripes, wide), lambda p, k: (0, p, 0, 0)
        ),
        out_shape=jax.ShapeDtypeStruct((stripes, groups, L // stripes, wide), BF),
        scratch_shapes=[
            pltpu.VMEM((levels * receivers, some * wide), BF),
            pltpu.VMEM((transmits, 8, some * wide), F32),
            pltpu.VMEM((L // 8, 8, some * wide), F32),
            pltpu.VMEM((block // 2 * L, levels * receivers), BF),
            pltpu.VMEM((block // 2 * L, levels * receivers), BF),
        ],
        compiler_params=pltpu.CompilerParams(vmem_limit_bytes=50 * 2**20),
        cost_estimate=pl.CostEstimate(
            flops=2 * transmits * levels * receivers * groups * wide * L,
            bytes_accessed=transmits * receivers * diff * 2,
            transcendentals=0,
        ),
    )(masks, delta, dsum, *tx_bits)


def on_device(sizes, encoded, signs, tx_block, rx_block, apodization):
    lines_here = rx_block.shape[1]
    stripes, groups = sizes
    events, transmits = signs.shape
    receivers = rx_block.shape[0]
    at = lax.axis_index("tx").astype(jnp.int32).reshape(1)
    masks, own, st = cast(sizes, at, rx_block, apodization, tx_block, signs.T)
    masks = lax.all_to_all(masks, "img", 0, 0, tiled=True)
    tx_bits = [own] + [
        lax.ppermute(own, "tx", [((t + d) % stripes, t) for t in range(stripes)])
        for d in range(1, stripes)
    ]
    delta, dsum = decode(st, encoded)
    delta = delta.reshape(transmits, *delta.shape[2:])
    scale = math.sqrt(events / (transmits * receivers)) / events
    parts = beamform(scale, stripes, masks, tx_bits, delta, dsum)
    parts = parts.reshape(stripes * groups, L // stripes, lines_here)
    parts = lax.all_to_all(parts, ("tx", "img"), 0, 0, tiled=True)
    return jnp.sum(parts.astype(F32), axis=0).T


def solution(mesh):
    placed = (P("tx", "img", None), P(), P("tx", None), P(None, "img"), P(None, "img"))
    sizes = (mesh.shape["tx"], mesh.shape["img"])
    return jax.shard_map(
        functools.partial(on_device, sizes),
        mesh=mesh, in_specs=placed, out_specs=P("img", "tx"), check_vma=False,
    )
```

```python
import functools
import math

import jax
import jax.numpy as jnp
from jax import lax
from jax.experimental import pallas as pl
from jax.experimental.pallas import tpu as pltpu
from jax.sharding import PartitionSpec as P

L = 128
G = 4
COPIES = 4
RB = 16
BF = jnp.bfloat16
F32 = jnp.float32


def iota(shape, axis):
    return lax.broadcasted_iota(jnp.int32, shape, axis)


def dot(a, b):
    return jnp.dot(a, b, preferred_element_type=F32)


def cast_kernel(
    stripes, at_ref, rx_ref, on_ref, tx_ref, sign_ref, out_ref, bits_ref, st_ref
):
    out_ref[:, 0] = rx_ref[...].astype(F32).astype(BF)
    out_ref[:, 1] = on_ref[...].astype(F32).astype(BF)

    @pl.when(pl.program_id(0) == 0)
    def _():
        bits_ref[...] = tx_ref[...].astype(F32).astype(BF)
        every = st_ref.shape[0]
        turn = at_ref[0] * (every // stripes)
        row = lax.rem(iota((every, every), 0) + turn, every)
        up = (row == iota((every, every), 1)).astype(F32).astype(BF)
        st_ref[...] = dot(up, sign_ref[...].astype(F32).astype(BF)).astype(BF)


def cast(sizes, at, rx_block, apodization, tx_block, signs_t):
    stripes, groups = sizes
    receivers, lines_here = rx_block.shape
    every, events = signs_t.shape
    here = receivers // groups
    split = (groups, here, lines_here)
    whole = pl.BlockSpec(tx_block.shape, lambda i, at: (0, 0))
    part = pl.BlockSpec((groups // 2, here, lines_here), lambda i, at: (i, 0, 0))
    return pl.pallas_call(
        functools.partial(cast_kernel, stripes),
        grid_spec=pltpu.PrefetchScalarGridSpec(
            num_scalar_prefetch=1,
            grid=(2,),
            in_specs=[
                part,
                part,
                whole,
                pl.BlockSpec((every, events // stripes), lambda i, at: (0, at[0])),
            ],
            out_specs=[
                pl.BlockSpec(
                    (groups // 2, 2, here, lines_here), lambda i, at: (i, 0, 0, 0)
                ),
                whole,
                pl.BlockSpec((every, events // stripes), lambda i, at: (0, 0)),
            ],
        ),
        out_shape=[
            jax.ShapeDtypeStruct((groups, 2, here, lines_here), BF),
            jax.ShapeDtypeStruct(tx_block.shape, BF),
            jax.ShapeDtypeStruct((every, events // stripes), BF),
        ],
    )(at, rx_block.reshape(split), apodization.reshape(split), tx_block, signs_t)


def decode_kernel(st_ref, *refs):
    *enc_refs, delta_ref, dsum_ref, sk_ref, x_ref = refs
    transmits, events = st_ref.shape
    share, _, samples = enc_refs[0].shape
    rows, depth = sk_ref.shape
    diff = samples - L
    width = 32

    @pl.when(pl.program_id(0) == 0)
    def _():
        up = iota((rows, transmits), 0) // G == iota((rows, transmits), 1)
        tall = dot(up.astype(F32).astype(BF), st_ref[...]).astype(BF)
        wide = 256
        for at in range(0, depth, wide):
            row = iota((events, wide), 1) + at
            event = row // RB * 4 + row // G % 2 * 2 + row // (2 * G) % 2
            out = event == iota((events, wide), 0)
            spread = dot(tall, out.astype(F32).astype(BF))
            same = iota((rows, wide), 0) % G == iota((rows, wide), 1) % G
            sk_ref[:, at : at + wide] = jnp.where(same, spread, 0.0).astype(BF)

    row = iota((1, RB, samples), 1)
    first, inner = row < 2 * G, row % (2 * G) < G
    for at in range(0, events, width):
        piece = enc_refs[at // share][at % share : at % share + width]
        piece = piece.reshape(width // 4, 4, RB, samples)
        a, b, c, d = (piece[:, e] for e in range(4))
        here = slice(at * G, (at + width) * G)
        for side in range(2):
            if side == 0:
                ab = jnp.where(first, a, pltpu.roll(b, 2 * G, 1))
                cd = jnp.where(first, c, pltpu.roll(d, 2 * G, 1))
            else:
                ab = jnp.where(first, pltpu.roll(a, 2 * G, 1), b)
                cd = jnp.where(first, pltpu.roll(c, 2 * G, 1), d)
            low = jnp.where(inner, ab, pltpu.roll(cd, G, 1))
            high = jnp.where(inner, pltpu.roll(ab, RB - G, 1), cd)
            x_ref[2 * side, here, :] = low.reshape(width * G, samples)
            x_ref[2 * side + 1, here, :] = high.reshape(width * G, samples)
    deltas = []
    for q in range(RB // G):
        d = dot(sk_ref[...], x_ref[q])
        low, high = d[:, :diff], d[:, L:]
        deltas.append(((high - low) * 0.5).reshape(transmits // 2, 2 * G, diff))
        mean = jnp.sum((high + low).reshape(transmits // 2, 2 * G, diff), axis=0)
        dsum_ref[q * G : (q + 1) * G, :] = (mean[:G] + mean[G:]) * 0.5
    upper = iota((1, 2 * G, diff), 1) < G
    evens, odds = [], []
    for side in range(2):
        low, high = deltas[2 * side], deltas[2 * side + 1]
        evens.append(jnp.where(upper, low, pltpu.roll(high, G, 1)))
        odds.append(jnp.where(upper, pltpu.roll(low, G, 1), high))
    delta_ref[:, 0] = jnp.concatenate(evens, axis=1).astype(BF)
    delta_ref[:, 1] = jnp.concatenate(odds, axis=1).astype(BF)


def decode(st, encoded):
    transmits, events = st.shape
    _, receivers, samples = encoded.shape
    diff = samples - L
    return pl.pallas_call(
        decode_kernel,
        grid=(receivers // RB,),
        in_specs=[
            pl.BlockSpec((transmits, events), lambda g: (0, 0)),
        ]
        + [
            pl.BlockSpec(
                (events // COPIES, RB, samples), functools.partial(lambda c, g: (c, g, 0), c)
            )
            for c in range(COPIES)
        ],
        out_specs=[
            pl.BlockSpec((transmits // 2, 2, RB, diff), lambda g: (0, 0, g, 0)),
            pl.BlockSpec((RB, diff), lambda g: (g, 0)),
        ],
        out_shape=[
            jax.ShapeDtypeStruct((transmits // 2, 2, receivers, diff), BF),
            jax.ShapeDtypeStruct((receivers, diff), F32),
        ],
        scratch_shapes=[
            pltpu.VMEM((transmits * G, events * G), BF),
            pltpu.VMEM((RB // G, events * G, samples), BF),
        ],
        compiler_params=pltpu.CompilerParams(vmem_limit_bytes=50 * 2**20),
        cost_estimate=pl.CostEstimate(
            flops=16 * transmits * events * receivers * samples,
            bytes_accessed=events * receivers * samples * 2
            + transmits * receivers * diff * 2,
            transcendentals=0,
        ),
    )(st, *[encoded] * COPIES)


def beam_kernel(scale, mask_ref, delta_ref, dsum_ref, *refs):
    *tx_refs, out_ref, a_ref, s_ref, acc_ref, even_ref, odd_ref = refs
    block, receivers, diff = delta_ref.shape
    levels = diff // L
    half = block // 2
    groups, _, _, wide = mask_ref.shape
    step, last = pl.program_id(1), pl.num_programs(1) - 1

    def turn(x_to, side, k):
        for v in range(levels):
            x_to[k * L : (k + 1) * L, v * receivers : (v + 1) * receivers] = delta_ref[
                side * half + k, :, v * L : (v + 1) * L
            ].T

    def product(x_from, k0, beside):
        for g in range(groups):
            for k in range(g * half // groups, (g + 1) * half // groups):
                beside(k)
            here = slice(g * wide, (g + 1) * wide)
            y = dot(x_from[...], a_ref[:, here]).reshape(half, L // 8, 8, wide)
            acc = acc_ref[:, :, here]
            for k in range(half):
                acc = acc + s_ref[k0 + k, :, here] * y[k]
            acc_ref[:, :, here] = acc

    @pl.when(step == 0)
    def _():
        for v in range(levels):
            whole = dsum_ref[:, v * L : (v + 1) * L]
            high = whole.astype(BF)
            here = slice(v * receivers, (v + 1) * receivers)
            odd_ref[:L, here] = high.T
            odd_ref[L : 2 * L, here] = (whole - high.astype(F32)).astype(BF).T
        for g in range(groups):
            here = slice(g * wide, (g + 1) * wide)
            rx, on = mask_ref[g, 0].astype(F32), mask_ref[g, 1].astype(F32)
            for v in range(levels):
                a_ref[v * receivers : (v + 1) * receivers, here] = jnp.where(
                    rx == v, on, 0.0
                ).astype(BF)
            y = dot(odd_ref[: 2 * L, :], a_ref[:, here])
            acc_ref[:, :, here] = (y[:L] + y[L:]).reshape(L // 8, 8, wide)
            at = 0
            for ref in tx_refs:
                s = 2.0 * ref[:, here].astype(F32) - 1.0
                for k in range(ref.shape[0]):
                    s_ref[at + k, :, here] = jnp.broadcast_to(s[k : k + 1], (8, wide))
                at += ref.shape[0]
        for k in range(half):
            turn(even_ref, 0, k)

    @pl.when(step > 0)
    def _():
        product(odd_ref, step * block - half, functools.partial(turn, even_ref, 0))

    @pl.when(step < last)
    def _():
        product(even_ref, step * block, functools.partial(turn, odd_ref, 1))

    @pl.when(step == last)
    def _():
        stripes, _, deep, _ = out_ref.shape
        for g in range(groups):
            here = slice(g * wide, (g + 1) * wide)
            whole = (acc_ref[:, :, here] * scale).reshape(L, wide)
            for t in range(stripes):
                out_ref[t, g] = whole[t * deep : (t + 1) * deep, :].astype(BF)


def beamform(scale, stripes, masks, tx_bits, delta, dsum):
    groups, _, receivers, wide = masks.shape
    transmits, _, diff = delta.shape
    levels = diff // L
    block = min(16, transmits)
    some = min(groups, 8)
    steps = transmits // block
    return pl.pallas_call(
        functools.partial(beam_kernel, scale),
        grid=(groups // some, steps + 1),
        in_specs=[
            pl.BlockSpec((some, 2, receivers, wide), lambda p, k: (p, 0, 0, 0)),
            pl.BlockSpec(
                (block, receivers, diff), lambda p, k: (jnp.minimum(k, steps - 1), 0, 0)
            ),
            pl.BlockSpec((receivers, diff), lambda p, k: (0, 0)),
        ]
        + [
            pl.BlockSpec((t.shape[0], some * wide), lambda p, k: (0, p))
            for t in tx_bits
        ],
        out_specs=pl.BlockSpec(
            (stripes, some, L // stripes, wide), lambda p, k: (0, p, 0, 0)
        ),
        out_shape=jax.ShapeDtypeStruct((stripes, groups, L // stripes, wide), BF),
        scratch_shapes=[
            pltpu.VMEM((levels * receivers, some * wide), BF),
            pltpu.VMEM((transmits, 8, some * wide), F32),
            pltpu.VMEM((L // 8, 8, some * wide), F32),
            pltpu.VMEM((block // 2 * L, levels * receivers), BF),
            pltpu.VMEM((block // 2 * L, levels * receivers), BF),
        ],
        compiler_params=pltpu.CompilerParams(vmem_limit_bytes=50 * 2**20),
        cost_estimate=pl.CostEstimate(
            flops=2 * transmits * levels * receivers * groups * wide * L,
            bytes_accessed=transmits * receivers * diff * 2,
            transcendentals=0,
        ),
    )(masks, delta, dsum, *tx_bits)


def on_device(sizes, encoded, signs, tx_block, rx_block, apodization):
    lines_here = rx_block.shape[1]
    stripes, groups = sizes
    events, transmits = signs.shape
    receivers = rx_block.shape[0]
    at = lax.axis_index("tx").astype(jnp.int32).reshape(1)
    masks, own, st = cast(sizes, at, rx_block, apodization, tx_block, signs.T)
    masks = lax.all_to_all(masks, "img", 0, 0, tiled=True)
    tx_bits = [own] + [
        lax.ppermute(own, "tx", [((t + d) % stripes, t) for t in range(stripes)])
        for d in range(1, stripes)
    ]
    delta, dsum = decode(st, encoded)
    delta = delta.reshape(transmits, *delta.shape[2:])
    scale = math.sqrt(events / (transmits * receivers)) / events
    parts = beamform(scale, stripes, masks, tx_bits, delta, dsum)
    parts = parts.reshape(stripes * groups, L // stripes, lines_here)
    parts = lax.all_to_all(parts, ("tx", "img"), 0, 0, tiled=True)
    return jnp.sum(parts.astype(F32), axis=0).T


def solution(mesh):
    placed = (P("tx", "img", None), P(), P("tx", None), P(None, "img"), P(None, "img"))
    sizes = (mesh.shape["tx"], mesh.shape["img"])
    return jax.shard_map(
        functools.partial(on_device, sizes),
        mesh=mesh, in_specs=placed, out_specs=P("img", "tx"), check_vma=False,
    )
```

```python
import functools
import math

import jax
import jax.numpy as jnp
from jax import lax
from jax.experimental import pallas as pl
from jax.experimental.pallas import tpu as pltpu
from jax.sharding import PartitionSpec as P

L = 128
G = 4
COPIES = 4
RB = 16
BF = jnp.bfloat16
F32 = jnp.float32


def iota(shape, axis):
    return lax.broadcasted_iota(jnp.int32, shape, axis)


def dot(a, b):
    return jnp.dot(a, b, preferred_element_type=F32)


def cast_kernel(
    stripes, at_ref, rx_ref, on_ref, tx_ref, sign_ref, out_ref, bits_ref, st_ref
):
    out_ref[:, 0] = rx_ref[...].astype(F32).astype(BF)
    out_ref[:, 1] = on_ref[...].astype(F32).astype(BF)

    @pl.when(pl.program_id(0) == 0)
    def _():
        bits_ref[...] = tx_ref[...].astype(F32).astype(BF)
        every = st_ref.shape[0]
        turn = at_ref[0] * (every // stripes)
        row = lax.rem(iota((every, every), 0) + turn, every)
        up = (row == iota((every, every), 1)).astype(F32).astype(BF)
        st_ref[...] = dot(up, sign_ref[...].astype(F32).astype(BF)).astype(BF)


def cast(sizes, at, rx_block, apodization, tx_block, signs_t):
    stripes, groups = sizes
    receivers, lines_here = rx_block.shape
    every, events = signs_t.shape
    here = receivers // groups
    split = (groups, here, lines_here)
    whole = pl.BlockSpec(tx_block.shape, lambda i, at: (0, 0))
    part = pl.BlockSpec((groups // 2, here, lines_here), lambda i, at: (i, 0, 0))
    return pl.pallas_call(
        functools.partial(cast_kernel, stripes),
        grid_spec=pltpu.PrefetchScalarGridSpec(
            num_scalar_prefetch=1,
            grid=(2,),
            in_specs=[
                part,
                part,
                whole,
                pl.BlockSpec((every, events // stripes), lambda i, at: (0, at[0])),
            ],
            out_specs=[
                pl.BlockSpec(
                    (groups // 2, 2, here, lines_here), lambda i, at: (i, 0, 0, 0)
                ),
                whole,
                pl.BlockSpec((every, events // stripes), lambda i, at: (0, 0)),
            ],
        ),
        out_shape=[
            jax.ShapeDtypeStruct((groups, 2, here, lines_here), BF),
            jax.ShapeDtypeStruct(tx_block.shape, BF),
            jax.ShapeDtypeStruct((every, events // stripes), BF),
        ],
    )(at, rx_block.reshape(split), apodization.reshape(split), tx_block, signs_t)


def decode_kernel(st_ref, *refs):
    *enc_refs, delta_ref, dsum_ref, sk_ref, x_ref = refs
    transmits, events = st_ref.shape
    share, _, samples = enc_refs[0].shape
    rows, depth = sk_ref.shape
    diff = samples - L
    width = 32

    @pl.when(pl.program_id(0) == 0)
    def _():
        up = iota((rows, transmits), 0) // G == iota((rows, transmits), 1)
        tall = dot(up.astype(F32).astype(BF), st_ref[...]).astype(BF)
        wide = 256
        for at in range(0, depth, wide):
            row = iota((events, wide), 1) + at
            event = row // RB * 4 + row // G % 2 * 2 + row // (2 * G) % 2
            out = event == iota((events, wide), 0)
            spread = dot(tall, out.astype(F32).astype(BF))
            same = iota((rows, wide), 0) % G == iota((rows, wide), 1) % G
            sk_ref[:, at : at + wide] = jnp.where(same, spread, 0.0).astype(BF)

    row = iota((1, RB, samples), 1)
    first, inner = row < 2 * G, row % (2 * G) < G
    for at in range(0, events, width):
        piece = enc_refs[at // share][at % share : at % share + width]
        piece = piece.reshape(width // 4, 4, RB, samples)
        a, b, c, d = (piece[:, e] for e in range(4))
        here = slice(at * G, (at + width) * G)
        for side in range(2):
            if side == 0:
                ab = jnp.where(first, a, pltpu.roll(b, 2 * G, 1))
                cd = jnp.where(first, c, pltpu.roll(d, 2 * G, 1))
            else:
                ab = jnp.where(first, pltpu.roll(a, 2 * G, 1), b)
                cd = jnp.where(first, pltpu.roll(c, 2 * G, 1), d)
            low = jnp.where(inner, ab, pltpu.roll(cd, G, 1))
            high = jnp.where(inner, pltpu.roll(ab, RB - G, 1), cd)
            x_ref[2 * side, here, :] = low.reshape(width * G, samples)
            x_ref[2 * side + 1, here, :] = high.reshape(width * G, samples)
    deltas = []
    for q in range(RB // G):
        d = dot(sk_ref[...], x_ref[q])
        low, high = d[:, :diff], d[:, L:]
        deltas.append(((high - low) * 0.5).reshape(transmits // 2, 2 * G, diff))
        mean = jnp.sum((high + low).reshape(transmits // 2, 2 * G, diff), axis=0)
        dsum_ref[q * G : (q + 1) * G, :] = (mean[:G] + mean[G:]) * 0.5
    upper = iota((1, 2 * G, diff), 1) < G
    evens, odds = [], []
    for side in range(2):
        low, high = deltas[2 * side], deltas[2 * side + 1]
        evens.append(jnp.where(upper, low, pltpu.roll(high, G, 1)))
        odds.append(jnp.where(upper, pltpu.roll(low, G, 1), high))
    delta_ref[:, 0] = jnp.concatenate(evens, axis=1).astype(BF)
    delta_ref[:, 1] = jnp.concatenate(odds, axis=1).astype(BF)


def decode(st, encoded):
    transmits, events = st.shape
    _, receivers, samples = encoded.shape
    diff = samples - L
    return pl.pallas_call(
        decode_kernel,
        grid=(receivers // RB,),
        in_specs=[
            pl.BlockSpec((transmits, events), lambda g: (0, 0)),
        ]
        + [
            pl.BlockSpec(
                (events // COPIES, RB, samples), functools.partial(lambda c, g: (c, g, 0), c)
            )
            for c in range(COPIES)
        ],
        out_specs=[
            pl.BlockSpec((transmits // 2, 2, RB, diff), lambda g: (0, 0, g, 0)),
            pl.BlockSpec((RB, diff), lambda g: (g, 0)),
        ],
        out_shape=[
            jax.ShapeDtypeStruct((transmits // 2, 2, receivers, diff), BF),
            jax.ShapeDtypeStruct((receivers, diff), F32),
        ],
        scratch_shapes=[
            pltpu.VMEM((transmits * G, events * G), BF),
            pltpu.VMEM((RB // G, events * G, samples), BF),
        ],
        compiler_params=pltpu.CompilerParams(vmem_limit_bytes=50 * 2**20),
        cost_estimate=pl.CostEstimate(
            flops=16 * transmits * events * receivers * samples,
            bytes_accessed=events * receivers * samples * 2
            + transmits * receivers * diff * 2,
            transcendentals=0,
        ),
    )(st, *[encoded] * COPIES)


def beam_kernel(scale, mask_ref, delta_ref, dsum_ref, *refs):
    *tx_refs, out_ref, a_ref, s_ref, acc_ref, even_ref, odd_ref = refs
    block, receivers, diff = delta_ref.shape
    levels = diff // L
    half = block // 2
    groups, _, _, wide = mask_ref.shape
    step, last = pl.program_id(1), pl.num_programs(1) - 1

    def turn(x_to, side, k):
        for v in range(levels):
            x_to[k * L : (k + 1) * L, v * receivers : (v + 1) * receivers] = delta_ref[
                side * half + k, :, v * L : (v + 1) * L
            ].T

    def product(x_from, k0, beside):
        for g in range(0, groups, 2):
            for k in range(g * half // groups, (g + 2) * half // groups):
                beside(k)
            here = slice(g * wide, (g + 2) * wide)
            y = dot(x_from[...], a_ref[:, here]).reshape(half, L // 8, 8, 2 * wide)
            acc = acc_ref[:, :, here]
            for k in range(half):
                acc = acc + s_ref[k0 + k, :, here] * y[k]
            acc_ref[:, :, here] = acc

    @pl.when(step == 0)
    def _():
        for v in range(levels):
            whole = dsum_ref[:, v * L : (v + 1) * L]
            high = whole.astype(BF)
            here = slice(v * receivers, (v + 1) * receivers)
            odd_ref[:L, here] = high.T
            odd_ref[L : 2 * L, here] = (whole - high.astype(F32)).astype(BF).T
        for g in range(groups):
            here = slice(g * wide, (g + 1) * wide)
            rx, on = mask_ref[g, 0].astype(F32), mask_ref[g, 1].astype(F32)
            for v in range(levels):
                a_ref[v * receivers : (v + 1) * receivers, here] = jnp.where(
                    rx == v, on, 0.0
                ).astype(BF)
            y = dot(odd_ref[: 2 * L, :], a_ref[:, here])
            acc_ref[:, :, here] = (y[:L] + y[L:]).reshape(L // 8, 8, wide)
            at = 0
            for ref in tx_refs:
                s = 2.0 * ref[:, here].astype(F32) - 1.0
                for k in range(ref.shape[0]):
                    s_ref[at + k, :, here] = jnp.broadcast_to(s[k : k + 1], (8, wide))
                at += ref.shape[0]
        for k in range(half):
            turn(even_ref, 0, k)

    @pl.when(step > 0)
    def _():
        product(odd_ref, step * block - half, functools.partial(turn, even_ref, 0))

    @pl.when(step < last)
    def _():
        product(even_ref, step * block, functools.partial(turn, odd_ref, 1))

    @pl.when(step == last)
    def _():
        stripes, _, deep, _ = out_ref.shape
        for g in range(groups):
            here = slice(g * wide, (g + 1) * wide)
            whole = (acc_ref[:, :, here] * scale).reshape(L, wide)
            for t in range(stripes):
                out_ref[t, g] = whole[t * deep : (t + 1) * deep, :].astype(BF)


def beamform(scale, stripes, masks, tx_bits, delta, dsum):
    groups, _, receivers, wide = masks.shape
    transmits, _, diff = delta.shape
    levels = diff // L
    block = min(16, transmits)
    some = min(groups, 8)
    steps = transmits // block
    return pl.pallas_call(
        functools.partial(beam_kernel, scale),
        grid=(groups // some, steps + 1),
        in_specs=[
            pl.BlockSpec((some, 2, receivers, wide), lambda p, k: (p, 0, 0, 0)),
            pl.BlockSpec(
                (block, receivers, diff), lambda p, k: (jnp.minimum(k, steps - 1), 0, 0)
            ),
            pl.BlockSpec((receivers, diff), lambda p, k: (0, 0)),
        ]
        + [
            pl.BlockSpec((t.shape[0], some * wide), lambda p, k: (0, p))
            for t in tx_bits
        ],
        out_specs=pl.BlockSpec(
            (stripes, some, L // stripes, wide), lambda p, k: (0, p, 0, 0)
        ),
        out_shape=jax.ShapeDtypeStruct((stripes, groups, L // stripes, wide), BF),
        scratch_shapes=[
            pltpu.VMEM((levels * receivers, some * wide), BF),
            pltpu.VMEM((transmits, 8, some * wide), F32),
            pltpu.VMEM((L // 8, 8, some * wide), F32),
            pltpu.VMEM((block // 2 * L, levels * receivers), BF),
            pltpu.VMEM((block // 2 * L, levels * receivers), BF),
        ],
        compiler_params=pltpu.CompilerParams(vmem_limit_bytes=50 * 2**20),
        cost_estimate=pl.CostEstimate(
            flops=2 * transmits * levels * receivers * groups * wide * L,
            bytes_accessed=transmits * receivers * diff * 2,
            transcendentals=0,
        ),
    )(masks, delta, dsum, *tx_bits)


def on_device(sizes, encoded, signs, tx_block, rx_block, apodization):
    lines_here = rx_block.shape[1]
    stripes, groups = sizes
    events, transmits = signs.shape
    receivers = rx_block.shape[0]
    at = lax.axis_index("tx").astype(jnp.int32).reshape(1)
    masks, own, st = cast(sizes, at, rx_block, apodization, tx_block, signs.T)
    masks = lax.all_to_all(masks, "img", 0, 0, tiled=True)
    tx_bits = [own] + [
        lax.ppermute(own, "tx", [((t + d) % stripes, t) for t in range(stripes)])
        for d in range(1, stripes)
    ]
    delta, dsum = decode(st, encoded)
    delta = delta.reshape(transmits, *delta.shape[2:])
    scale = math.sqrt(events / (transmits * receivers)) / events
    parts = beamform(scale, stripes, masks, tx_bits, delta, dsum)
    parts = parts.reshape(stripes * groups, L // stripes, lines_here)
    parts = lax.all_to_all(parts, ("tx", "img"), 0, 0, tiled=True)
    return jnp.sum(parts.astype(F32), axis=0).T


def solution(mesh):
    placed = (P("tx", "img", None), P(), P("tx", None), P(None, "img"), P(None, "img"))
    sizes = (mesh.shape["tx"], mesh.shape["img"])
    return jax.shard_map(
        functools.partial(on_device, sizes),
        mesh=mesh, in_specs=placed, out_specs=P("img", "tx"), check_vma=False,
    )
```
